32 devices in a mesh: seq: 8 (over z, y), head: 4 (over x, core).
Axes of the slice: x: 2, y: 2, z: 4, core: 2. Of those that a mesh axis runs over, the one named last changes fastest.
Arguments:
- queries: bfloat16 [4096, 4096], P('seq', 'head'), may hold values from -60 to 60
- keys: bfloat16 [4096, 4096], P('seq', 'head'), may hold values from -8 to 8
- values: bfloat16 [4096, 4096], P('seq', 'head'), may hold values from -3000 to 3000
- gain: float32 [4096], P('head'), may hold values from 0.5 to 1.5
- grad_out: bfloat16 [4096, 4096], P('seq', 'head'), may hold values from -6 to 6
- pattern: int32 [32, 10], replicated, may hold values from 0 to 31, as said below
Outputs:
- normed: bfloat16 [4096, 4096], P('seq', 'head')
- grad_queries: bfloat16 [4096, 4096], P('seq', 'head')
- grad_keys: bfloat16 [4096, 4096], P('seq', 'head')
- grad_values: bfloat16 [4096, 4096], P('seq', 'head')
The draws below stay inside these ranges and needn't reach their ends.
Inputs may be any that keep to these rules, and one draw needn't show every extreme that they name: `pattern`: row g lists 10 distinct blocks: g itself, then 3 - 1 further blocks of g's range, then 7 blocks of other ranges. All blocks of a range s that rows of other ranges list are one block, s's export, and each range's export is listed by some row of another range.
All inputs are finite; a program needn't handle non-finite values.
Results may differ from the reference program's by a relative error of at most 0.012.
Values may be sent and summed in bfloat16 or wider, within the bound.
No kernel may reach another device: no remote copies, remote signals or barrier semaphores. Data moves between devices by JAX's collectives and lax.ppermute only.
A program may use at most 192 MiB of HBM per device.

```python
import math
import jax
import jax.numpy as jnp
from jax import lax

H = 32
HEAD_SIZE = 128
BLK = 128
KPB = 10
LOC = 3
REM = 7
FEAT = 4096
NB_DEV = 4
NBLK = 32
TOKENS = 4096
N_SEQ = 8


def alignment(key):
    base_keys = jnp.clip(jax.random.normal(jax.random.fold_in(key, 11), (TOKENS, FEAT), jnp.float32), -6.0, 6.0)
    return base_keys


def draw_keys(key, part):
    return alignment(key).astype(jnp.bfloat16)


def draw_queries(key, part):
    return jnp.clip(jax.random.normal(jax.random.fold_in(key, 16), (TOKENS, FEAT), jnp.float32), -6.0, 6.0).astype(jnp.bfloat16)


def draw_values(key, part):
    rise = (jnp.arange(FEAT) // HEAD_SIZE).astype(jnp.float32) / (H - 1)
    column = jnp.exp(jax.random.uniform(jax.random.fold_in(key, 21), (FEAT,), jnp.float32, 0.0, math.log(3.5)))
    base = jnp.clip(jax.random.normal(jax.random.fold_in(key, 23), (TOKENS, FEAT), jnp.float32), -6.0, 6.0)
    column = column * jnp.exp(rise * math.log(3.0))
    row = jnp.exp(jax.random.uniform(jax.random.fold_in(key, 22), (TOKENS, 1), jnp.float32, 0.0, math.log(10.0)))
    return (base * row * column).astype(jnp.bfloat16)


def shuffle_rows(key, rows, count):
    return jax.vmap(lambda single_key: jax.random.permutation(single_key, count))(jax.random.split(key, rows))


def draw_pattern(key, part):
    nranges = NBLK // NB_DEV
    ranges_of = jnp.arange(NBLK, dtype=jnp.int32) // NB_DEV
    inside = jnp.arange(NBLK, dtype=jnp.int32) % NB_DEV
    counts = jax.random.randint(jax.random.fold_in(key, 31), (nranges,), REM, nranges)
    offsets = jnp.concatenate([jnp.ones((nranges, 1), jnp.int32), shuffle_rows(jax.random.fold_in(key, 32), nranges, nranges - 2).astype(jnp.int32) + 2], axis=1)
    exports = jax.random.randint(jax.random.fold_in(key, 33), (nranges,), 0, NB_DEV)
    local_shift = shuffle_rows(jax.random.fold_in(key, 34), NBLK, NB_DEV - 1).astype(jnp.int32)[:, :LOC - 1] + 1
    local = ranges_of[:, None] * NB_DEV + (inside[:, None] + local_shift) % NB_DEV
    position = (inside[:, None] * REM + jnp.arange(REM, dtype=jnp.int32)[None, :]) % counts[ranges_of][:, None]
    sources = (ranges_of[:, None] + jnp.take_along_axis(offsets[ranges_of], position, axis=1)) % nranges
    remote = sources * NB_DEV + exports[sources]
    own = (ranges_of * NB_DEV + inside)[:, None]
    return jnp.concatenate([own, local, remote], axis=1).astype(jnp.int32)


def level_of(rng, dims, cuts, smallest, high):
    def one(axis_at, blocks):
        draws = jax.random.uniform(jax.random.fold_in(jax.random.fold_in(rng, 6), axis_at), (blocks,), jnp.float32, smallest / len(cuts), high / len(cuts))
        return jnp.repeat(jnp.exp(draws), dims[axis_at] // blocks).reshape((-1,) + (1,) * (len(dims) - axis_at - 1))

    level = one(*cuts[0])
    for cut in cuts[1:]:
        level = level * one(*cut)
    return level


def noise(rng, shape, deviation, bound, cuts=(), kind=jnp.bfloat16):
    result = deviation * jax.random.normal(rng, shape, jnp.float32)
    if cuts:
        result = result * level_of(rng, shape, cuts, -0.22, 0.18)
    return jnp.clip(result, -bound, bound).astype(kind)


def setup_inputs(seed: int = 0) -> dict:
    key_of = jax.random.split(jax.random.key(seed), 7)
    queries = draw_queries(jax.random.fold_in(key_of[6], 71), 0)
    keys = draw_keys(jax.random.fold_in(key_of[6], 71), 0)
    values = draw_values(jax.random.fold_in(key_of[6], 71), 0)
    gain = jnp.clip(1.0 + 0.1 * jax.random.normal(key_of[3], (FEAT,), jnp.float32), 0.5, 1.5)
    grad_out = noise(key_of[4], (TOKENS, FEAT), 1.0, 6.0, ((0, 8), (1, 4)))
    pattern = draw_pattern(jax.random.fold_in(key_of[6], 71), 0)
    return {"queries": queries, "keys": keys, "values": values, "gain": gain, "grad_out": grad_out, "pattern": pattern}


epsilon = 1e-06

def rounded_values(value):
    return lax.optimization_barrier(value.astype(jnp.bfloat16)).astype(jnp.float32)

def reference(queries, keys, values, gain, grad_out, pattern):
    nblocks = pattern.shape[0]
    softmax_scale = 1.0 / HEAD_SIZE ** 0.5
    owner = pattern // NB_DEV
    row_range = (jnp.arange(nblocks, dtype=jnp.int32) // NB_DEV)[:, None]
    remote = owner != row_range
    ranges = jnp.arange(N_SEQ, dtype=jnp.int32)
    exports = lax.optimization_barrier(jnp.max(jnp.where(remote[None] & (owner[None] == ranges[:, None, None]), pattern[None], -1), axis=(1, 2)))
    pair_index = (row_range * N_SEQ + owner).reshape(-1)
    flat_pattern = pattern.reshape(-1)
    local_mask = jnp.logical_not(remote).reshape(-1, 1, 1)

    def head_slice(array, head_number):
        piece = lax.dynamic_slice_in_dim(array, head_number * HEAD_SIZE, HEAD_SIZE, 1)
        return piece.astype(jnp.float32).reshape(nblocks, BLK, HEAD_SIZE)

    def listed_items(array, head_number):
        return head_slice(array, head_number)[pattern].reshape(nblocks, KPB * BLK, HEAD_SIZE)

    def probabilities(head_queries, listed_keys):
        logit_scores = jnp.einsum('zwr,zyr->zwy', head_queries, listed_keys) * softmax_scale
        peak = lax.optimization_barrier(jnp.max(logit_scores, axis=-1, keepdims=True))
        expo = jnp.exp(logit_scores - peak)
        return expo / lax.optimization_barrier(jnp.sum(expo, axis=-1, keepdims=True))

    def forward_head(head_number):
        attention_weights = probabilities(head_slice(queries, head_number), listed_items(keys, head_number))
        output_rows = jnp.einsum('jwv,jvy->jwy', rounded_values(attention_weights), listed_items(values, head_number))
        return output_rows.reshape(nblocks * BLK, HEAD_SIZE)
    attended = lax.map(forward_head, jnp.arange(H, dtype=jnp.int32))
    gain_heads = gain.astype(jnp.float32).reshape(H, 1, HEAD_SIZE)
    grad_heads = grad_out.astype(jnp.float32).reshape(-1, H, HEAD_SIZE).transpose(1, 0, 2)
    squares = lax.optimization_barrier(jnp.sum(attended * attended, axis=(0, 2)))
    scaled_grad = gain_heads * grad_heads
    cross = lax.optimization_barrier(jnp.sum(scaled_grad * attended, axis=(0, 2)))
    inverse = lax.rsqrt(squares / FEAT + epsilon)[None, :, None]
    normed = (attended * inverse * gain_heads).astype(jnp.bfloat16)
    normed = normed.transpose(1, 0, 2).reshape(-1, FEAT)
    d_attended = (inverse * scaled_grad - attended * inverse ** 3 * cross[None, :, None] / FEAT).astype(jnp.bfloat16)

    def combine(terms):
        terms = terms.reshape(nblocks * KPB, BLK, HEAD_SIZE)
        local_sum = jax.ops.segment_sum(jnp.where(local_mask, terms, 0.0), flat_pattern, num_segments=nblocks)
        pair_sum = jax.ops.segment_sum(jnp.where(local_mask, 0.0, terms), pair_index, num_segments=N_SEQ * N_SEQ)
        incoming = lax.optimization_barrier(jnp.sum(rounded_values(pair_sum).reshape(N_SEQ, N_SEQ, BLK, HEAD_SIZE), axis=0))
        total = local_sum.at[exports].add(incoming)
        return total.astype(jnp.bfloat16).reshape(-1, HEAD_SIZE)

    def backward_head(head_number):
        head_queries = head_slice(queries, head_number)
        listed_keys = listed_items(keys, head_number)
        listed_values = listed_items(values, head_number)
        attention_weights = probabilities(head_queries, listed_keys)
        block_gradient = d_attended[head_number].astype(jnp.float32).reshape(nblocks, BLK, HEAD_SIZE)
        out_block = attended[head_number].reshape(nblocks, BLK, HEAD_SIZE)
        delta = lax.optimization_barrier(jnp.sum(block_gradient * out_block, axis=-1, keepdims=True))
        probability_gradient = jnp.einsum('zwr,zyr->zwy', block_gradient, listed_values)
        score_gradient = rounded_values(attention_weights * (probability_gradient - delta))
        query_gradient = (softmax_scale * jnp.einsum('jwv,jvy->jwy', score_gradient, listed_keys)).astype(jnp.bfloat16).reshape(-1, HEAD_SIZE)
        key_summands = softmax_scale * jnp.einsum('wip,wio->wpo', score_gradient, head_queries)
        value_summands = jnp.einsum('wip,wio->wpo', rounded_values(attention_weights), block_gradient)
        return (query_gradient, combine(key_summands), combine(value_summands))
    grad_q, grad_k, grad_v = lax.map(backward_head, jnp.arange(H, dtype=jnp.int32))
    grad_q = grad_q.transpose(1, 0, 2).reshape(-1, FEAT)
    grad_k = grad_k.transpose(1, 0, 2).reshape(-1, FEAT)
    grad_v = grad_v.transpose(1, 0, 2).reshape(-1, FEAT)
    return (normed, grad_q, grad_k, grad_v)
```

```python
import functools

import jax
import jax.numpy as jnp
from jax import lax
from jax.experimental import pallas as pl
from jax.experimental.pallas import tpu as pltpu
from jax.sharding import PartitionSpec as P

HEAD_SIZE = 128
BLK = 128
LOC = 3
REM = 7
FEAT = 4096
LOW = -1e30

epsilon = 1e-06
softmax_scale = 1.0 / HEAD_SIZE**0.5

NT = (((1,), (1,)), ((), ()))
NN = (((1,), (0,)), ((), ()))
TN = (((0,), (0,)), ((), ()))


def dot(a, b, dims):
    return lax.dot_general(a, b, dims, preferred_element_type=jnp.float32)


def softmax_kernel(nblocks, masked, bias_ref, q_ref, local_ref, *refs):
    slots = refs[:-2]
    p_ref, cat_ref = refs[-2:]
    tokens = q_ref.shape[0]
    cat_ref[:tokens] = local_ref[...]
    for j, slot in enumerate(slots):
        cat_ref[tokens + j * BLK : tokens + (j + 1) * BLK] = slot[...]
    for g in range(nblocks):
        rows = slice(g * BLK, (g + 1) * BLK)
        scores = dot(q_ref[rows], cat_ref[...], NT) * softmax_scale
        parts = []
        for j in range(nblocks + len(slots)):
            part = scores[:, j * BLK : (j + 1) * BLK]
            if j < nblocks or masked:
                part = part + bias_ref[g, j]
            parts.append(part)
        scores = jnp.concatenate(parts, axis=1)
        peak = jnp.max(scores, axis=1, keepdims=True)
        expo = jnp.exp(scores - peak)
        total = jnp.sum(expo, axis=1, keepdims=True)
        p_ref[0, rows] = (expo * (1.0 / total)).astype(p_ref.dtype)


def attend_kernel(p_ref, local_ref, grad_ref, gain_ref, *refs):
    slots = refs[:-5]
    o_ref, stat_ref, cat_ref, square_ref, cross_ref = refs[-5:]
    head = pl.program_id(0)
    tokens = local_ref.shape[0]
    cat_ref[:tokens] = local_ref[...]
    for j, slot in enumerate(slots):
        cat_ref[tokens + j * BLK : tokens + (j + 1) * BLK] = slot[...]
    out = dot(p_ref[0], cat_ref[...], NN)
    o_ref[...] = out
    scaled = grad_ref[...].astype(jnp.float32) * gain_ref[...]

    @pl.when(head == 0)
    def _():
        square_ref[...] = jnp.zeros_like(square_ref)
        cross_ref[...] = jnp.zeros_like(cross_ref)

    square_ref[...] += out * out
    cross_ref[...] += scaled * out

    @pl.when(head == pl.num_programs(0) - 1)
    def _():
        ones = jnp.ones((8, HEAD_SIZE), jnp.float32)
        total = functools.partial(
            lax.dot_general,
            ones,
            dimension_numbers=NT,
            precision=lax.Precision.HIGHEST,
            preferred_element_type=jnp.float32,
        )
        row = lax.broadcasted_iota(jnp.int32, stat_ref.shape, 0)
        stat_ref[...] = jnp.where(row == 0, total(square_ref[...]), total(cross_ref[...]))


def value_kernel(nblocks, nslots, start_ref, stat_ref, o_ref, grad_ref, gain_ref, p_ref, *refs):
    normed_ref, d_ref, local_ref, export_ref = refs[:4]
    slots = refs[4 : 4 + nslots]
    inverse_ref, factor_ref, term_ref = refs[4 + nslots :]
    tokens = o_ref.shape[0]

    @pl.when(pl.program_id(0) == 0)
    def _():
        stats = jnp.sum(stat_ref[...], axis=0)
        squares = jnp.broadcast_to(stats[0:1], (HEAD_SIZE, tokens)).T
        cross = jnp.broadcast_to(stats[1:2], (HEAD_SIZE, tokens)).T
        inverse = lax.rsqrt(squares / FEAT + epsilon)
        inverse_ref[...] = inverse
        factor_ref[...] = inverse * inverse * inverse * cross / FEAT

    out = o_ref[...]
    inverse = inverse_ref[...]
    gain = gain_ref[...]
    scaled = grad_ref[...].astype(jnp.float32) * gain
    normed_ref[...] = (out * inverse * gain).astype(normed_ref.dtype)
    d_attended = (inverse * scaled - out * factor_ref[...]).astype(d_ref.dtype)
    d_ref[...] = d_attended
    for j in range(nslots):
        cols = slice(tokens + j * BLK, tokens + (j + 1) * BLK)
        slots[j][...] = dot(p_ref[0, :, cols], d_attended, TN).astype(slots[j].dtype)
    term_ref[...] = dot(p_ref[0, :, :tokens], d_attended, TN)
    local_ref[...] = term_ref[...].astype(local_ref.dtype)
    start = pl.multiple_of(start_ref[0], BLK)
    export_ref[...] = term_ref[pl.ds(start, BLK)]


def key_kernel(nblocks, nslots, start_ref, q_ref, k_ref, v_ref, o_ref, d_ref, p_ref, *refs):
    key_in = refs[:nslots]
    value_in = refs[nslots : 2 * nslots]
    dq_ref, local_ref, export_ref = refs[2 * nslots : 2 * nslots + 3]
    slots = refs[2 * nslots + 3 : 3 * nslots + 3]
    key_cat, value_cat, score_ref, term_ref = refs[3 * nslots + 3 :]
    tokens = q_ref.shape[0]
    key_cat[:tokens] = k_ref[...]
    value_cat[:tokens] = v_ref[...]
    for j in range(nslots):
        rows = slice(tokens + j * BLK, tokens + (j + 1) * BLK)
        key_cat[rows] = key_in[j][...]
        value_cat[rows] = value_in[j][...]
    for g in range(nblocks):
        rows = slice(g * BLK, (g + 1) * BLK)
        d_attended = d_ref[rows]
        delta = jnp.sum(d_attended.astype(jnp.float32) * o_ref[rows], axis=1, keepdims=True)
        dprob = dot(d_attended, value_cat[...], NT)
        dscore = p_ref[0, rows].astype(jnp.float32) * (dprob - delta)
        dscore = dscore.astype(jnp.bfloat16)
        score_ref[rows] = dscore
        dq_ref[rows] = (dot(dscore, key_cat[...], NN) * softmax_scale).astype(dq_ref.dtype)
    for j in range(nslots):
        cols = slice(tokens + j * BLK, tokens + (j + 1) * BLK)
        term = dot(score_ref[:, cols], q_ref[...], TN) * softmax_scale
        slots[j][...] = term.astype(slots[j].dtype)
    term_ref[...] = dot(score_ref[:, :tokens], q_ref[...], TN) * softmax_scale
    local_ref[...] = term_ref[...].astype(local_ref.dtype)
    start = pl.multiple_of(start_ref[0], BLK)
    export_ref[...] = term_ref[pl.ds(start, BLK)]


def column(rows):
    return pl.BlockSpec((rows, HEAD_SIZE), lambda h, *_: (0, h))


def shards(queries, keys, values, gain, grad_out, pattern):
    n_seq = lax.axis_size("seq")
    far = n_seq // 2
    myself = lax.axis_index("seq")
    tokens, width = queries.shape
    heads = width // HEAD_SIZE
    nblocks = tokens // BLK
    nslots = n_seq - 1
    span = tokens + nslots * BLK
    masked = nslots != REM

    def turn(x, k):
        pairs = [
            (a * 2 + b, (a + k) % far * 2 + b) for a in range(far) for b in range(2)
        ]
        return lax.ppermute(x, "seq", pairs)

    def swap(x):
        return lax.ppermute(x, "seq", [(i, i ^ 1) for i in range(n_seq)])

    owner = pattern // nblocks
    row_range = (jnp.arange(pattern.shape[0], dtype=jnp.int32) // nblocks)[:, None]
    mine = jnp.where((owner != row_range) & (owner == myself), pattern, -1)
    start = (jnp.max(mine) - myself * nblocks) * BLK
    key_export = lax.dynamic_slice_in_dim(keys, start, BLK, 0)
    value_export = lax.dynamic_slice_in_dim(values, start, BLK, 0)

    shifts = list(range(1, far))
    mates_k = [swap(key_export)]
    key_near = [turn(key_export, k) for k in shifts]
    value_export, key_near = lax.optimization_barrier((value_export, key_near))
    mates_v = [swap(value_export)]
    value_near = [turn(value_export, k) for k in shifts]
    mates_k += [swap(x) for x in key_near]
    mates_v += [swap(x) for x in value_near]
    key_slots = key_near + mates_k
    value_slots = value_near + mates_v

    a, b = myself // 2, myself % 2
    ranges = [(a - k) % far * 2 + b for k in shifts] + [
        (a - k) % far * 2 + 1 - b for k in range(far)
    ]
    my_rows = lax.dynamic_slice_in_dim(pattern, myself * nblocks, nblocks, 0)
    names = jnp.arange(nblocks, dtype=jnp.int32) + myself * nblocks
    listed = jnp.any(my_rows[:, :LOC, None] == names[None, None], axis=1)
    if masked:
        sources = jnp.stack(ranges)
        listed_far = jnp.any((my_rows[:, LOC:] // nblocks)[:, :, None] == sources, axis=1)
        listed = jnp.concatenate([listed, listed_far], axis=1)
    bias = jnp.where(listed, 0.0, LOW).astype(jnp.float32)

    flops = 2 * heads * tokens * span * HEAD_SIZE
    smem = pl.BlockSpec(memory_space=pltpu.SMEM)
    whole = column(tokens)
    block = column(BLK)
    prob_spec = pl.BlockSpec((1, tokens, span), lambda h, *_: (h, 0, 0))
    gain_spec = pl.BlockSpec((1, HEAD_SIZE), lambda h, *_: (0, h))
    params = pltpu.CompilerParams(vmem_limit_bytes=40 * 1024 * 1024)
    gain_row = gain.reshape(1, width)

    prob = pl.pallas_call(
        functools.partial(softmax_kernel, nblocks, masked),
        grid=(heads,),
        in_specs=[smem, whole, whole] + [block] * nslots,
        out_specs=prob_spec,
        out_shape=jax.ShapeDtypeStruct((heads, tokens, span), jnp.bfloat16),
        scratch_shapes=[pltpu.VMEM((span, HEAD_SIZE), jnp.bfloat16)],
        compiler_params=params,
        cost_estimate=pl.CostEstimate(
            flops=flops, bytes_accessed=16 * tokens * span, transcendentals=heads * tokens * span
        ),
        name="softmax",
    )(bias, queries, keys, *key_slots)

    attended, stats = pl.pallas_call(
        attend_kernel,
        grid=(heads,),
        in_specs=[prob_spec, whole, whole, gain_spec] + [block] * nslots,
        out_specs=[whole, pl.BlockSpec((8, tokens), lambda h: (0, 0))],
        out_shape=[
            jax.ShapeDtypeStruct((tokens, width), jnp.float32),
            jax.ShapeDtypeStruct((8, tokens), jnp.float32),
        ],
        scratch_shapes=[
            pltpu.VMEM((span, HEAD_SIZE), jnp.bfloat16),
            pltpu.VMEM((tokens, HEAD_SIZE), jnp.float32),
            pltpu.VMEM((tokens, HEAD_SIZE), jnp.float32),
        ],
        compiler_params=params,
        cost_estimate=pl.CostEstimate(
            flops=flops, bytes_accessed=16 * tokens * span, transcendentals=0
        ),
        name="attend",
    )(prob, values, grad_out, gain_row, *value_slots)

    stats = lax.all_gather(stats, "head")

    start_vec = start.reshape(1)
    local_shapes = [
        jax.ShapeDtypeStruct((tokens, width), jnp.bfloat16),
        jax.ShapeDtypeStruct((BLK, width), jnp.float32),
    ]
    slot_shapes = [jax.ShapeDtypeStruct((BLK, width), jnp.bfloat16)] * nslots
    normed, d_attended, value_local, value_mine, *value_terms = pl.pallas_call(
        functools.partial(value_kernel, nblocks, nslots),
        grid=(heads,),
        in_specs=[
            smem,
            pl.BlockSpec(stats.shape, lambda h: (0, 0, 0)),
            whole,
            whole,
            gain_spec,
            prob_spec,
        ],
        out_specs=[whole, whole, whole, block] + [block] * nslots,
        out_shape=[jax.ShapeDtypeStruct((tokens, width), jnp.bfloat16)] * 2
        + local_shapes
        + slot_shapes,
        scratch_shapes=[pltpu.VMEM((tokens, HEAD_SIZE), jnp.float32)] * 3,
        compiler_params=params,
        cost_estimate=pl.CostEstimate(
            flops=flops, bytes_accessed=16 * tokens * span, transcendentals=0
        ),
        name="value_terms",
    )(start_vec, stats, attended, grad_out, gain_row, prob)

    grad_queries, key_local, key_mine, *key_terms = pl.pallas_call(
        functools.partial(key_kernel, nblocks, nslots),
        grid=(heads,),
        in_specs=[smem, whole, whole, whole, whole, whole, prob_spec] + [block] * (2 * nslots),
        out_specs=[whole, whole, block] + [block] * nslots,
        out_shape=[jax.ShapeDtypeStruct((tokens, width), jnp.bfloat16)]
        + local_shapes
        + slot_shapes,
        scratch_shapes=[
            pltpu.VMEM((span, HEAD_SIZE), jnp.bfloat16),
            pltpu.VMEM((span, HEAD_SIZE), jnp.bfloat16),
            pltpu.VMEM((tokens, span), jnp.bfloat16),
            pltpu.VMEM((tokens, HEAD_SIZE), jnp.float32),
        ],
        compiler_params=params,
        cost_estimate=pl.CostEstimate(
            flops=3 * flops, bytes_accessed=16 * tokens * span, transcendentals=0
        ),
        name="key_terms",
    )(
        start_vec,
        queries,
        keys,
        values,
        attended,
        d_attended,
        prob,
        *key_slots,
        *value_slots,
    )

    def send_back(terms, own):
        near, mates = terms[: far - 1], terms[far - 1 :]
        total = own
        for k in shifts:
            crossed = swap(mates[k]).astype(jnp.float32) + near[k - 1].astype(jnp.float32)
            total = total + turn(crossed.astype(jnp.bfloat16), -k).astype(jnp.float32)
        return (total + swap(mates[0]).astype(jnp.float32)).astype(jnp.bfloat16)

    grad_values = lax.dynamic_update_slice_in_dim(
        value_local, send_back(value_terms, value_mine), start, 0
    )
    grad_keys = lax.dynamic_update_slice_in_dim(
        key_local, send_back(key_terms, key_mine), start, 0
    )
    return normed, grad_queries, grad_keys, grad_values


def solution(mesh):
    split = P("seq", "head")
    return jax.shard_map(
        shards,
        mesh=mesh,
        in_specs=(split, split, split, P("head"), split, P()),
        out_specs=(split, split, split, split),
        check_vma=False,
    )
```

```python
import functools

import jax
import jax.numpy as jnp
from jax import lax
from jax.experimental import pallas as pl
from jax.experimental.pallas import tpu as pltpu
from jax.sharding import PartitionSpec as P

HEAD_SIZE = 128
BLK = 128
LOC = 3
REM = 7
FEAT = 4096
LOW = -1e30

epsilon = 1e-06
softmax_scale = 1.0 / HEAD_SIZE**0.5

NT = (((1,), (1,)), ((), ()))
NN = (((1,), (0,)), ((), ()))
TN = (((0,), (0,)), ((), ()))


def dot(a, b, dims):
    return lax.dot_general(a, b, dims, preferred_element_type=jnp.float32)


def head_columns(h):
    return pl.ds(pl.multiple_of(h * HEAD_SIZE, HEAD_SIZE), HEAD_SIZE)


def pick_kernel(nblocks, me_ref, pattern_ref, key_ref, value_ref, key_out, value_out, both_out, start_ref):
    pattern = pattern_ref[...]
    low = me_ref[0] * nblocks
    row = lax.broadcasted_iota(jnp.int32, pattern.shape, 0)
    inside = (pattern >= low) & (pattern < low + nblocks)
    others = (row < low) | (row >= low + nblocks)
    offset = jnp.where(inside & others, pattern - low, 0).astype(jnp.float32)
    start = pl.multiple_of(jnp.max(offset).astype(jnp.int32) * BLK, BLK)
    start_ref[0] = start
    key_out[...] = key_ref[pl.ds(start, BLK)]
    value_out[...] = value_ref[pl.ds(start, BLK)]
    both_out[:BLK] = key_ref[pl.ds(start, BLK)]
    both_out[BLK:] = value_ref[pl.ds(start, BLK)]


def gather_rows(cat_ref, pieces, cols):
    at = 0
    for piece in pieces:
        rows = piece.shape[0]
        cat_ref[at : at + rows] = piece[:, cols]
        at += rows


def softmax_kernel(nblocks, split, ranges_ref, pattern_ref, q_ref, *refs):
    pieces = refs[:-3]
    pa_ref, pb_ref, cat_ref = refs[-3:]
    low = ranges_ref[0] * nblocks
    imported = cat_ref.shape[0] // BLK - nblocks

    def bias(g, j):
        listed = None
        if j < nblocks:
            for i in range(LOC):
                same = pattern_ref[low + g, i] == low + j
                listed = same if listed is None else listed | same
        elif imported != REM:
            for i in range(LOC, LOC + REM):
                same = pattern_ref[low + g, i] // nblocks == ranges_ref[1 + j - nblocks]
                listed = same if listed is None else listed | same
        return None if listed is None else jnp.where(listed, 0.0, LOW)

    biases = [[bias(g, j) for j in range(nblocks + imported)] for g in range(nblocks)]

    @pl.loop(0, pa_ref.shape[0])
    def _(h):
        cols = head_columns(h)
        gather_rows(cat_ref, pieces, cols)
        for g in range(nblocks):
            rows = slice(g * BLK, (g + 1) * BLK)
            scores = dot(q_ref[rows, cols], cat_ref[...], NT) * softmax_scale
            parts = []
            for j in range(nblocks + imported):
                part = scores[:, j * BLK : (j + 1) * BLK]
                if biases[g][j] is not None:
                    part = part + biases[g][j]
                parts.append(part)
            scores = jnp.concatenate(parts, axis=1)
            peak = jnp.max(scores, axis=1, keepdims=True)
            expo = jnp.exp(scores - peak)
            total = jnp.sum(expo, axis=1, keepdims=True)
            prob = (expo * (1.0 / total)).astype(pa_ref.dtype)
            pa_ref[h, rows] = prob[:, :split]
            pb_ref[h, rows] = prob[:, split:]


def attend_kernel(p_ref, *refs):
    pieces = refs[:-2]
    o_ref, cat_ref = refs[-2:]

    @pl.loop(0, p_ref.shape[0])
    def _(h):
        cols = head_columns(h)
        gather_rows(cat_ref, pieces, cols)
        o_ref[:, cols] = dot(p_ref[h], cat_ref[...], NN)


def attend_rest_kernel(p_ref, o_in, grad_ref, gain_ref, *refs):
    pieces = refs[:-5]
    o_ref, stat_ref, cat_ref, square_ref, cross_ref = refs[-5:]
    square_ref[...] = jnp.zeros_like(square_ref)
    cross_ref[...] = jnp.zeros_like(cross_ref)

    @pl.loop(0, p_ref.shape[0])
    def _(h):
        cols = head_columns(h)
        gather_rows(cat_ref, pieces, cols)
        out = o_in[:, cols] + dot(p_ref[h], cat_ref[...], NN)
        o_ref[:, cols] = out
        scaled = grad_ref[:, cols].astype(jnp.float32) * gain_ref[:, cols]
        square_ref[...] += out * out
        cross_ref[...] += scaled * out

    stat_ref[0:1] = jnp.sum(square_ref[...].T, axis=0, keepdims=True)
    stat_ref[1:2] = jnp.sum(cross_ref[...].T, axis=0, keepdims=True)
    stat_ref[2:] = jnp.zeros_like(stat_ref[2:])


def put_terms(scores, right, slots, first, cols, scale):
    for j, slot in enumerate(slots):
        part = slice(first + j * BLK, first + (j + 1) * BLK)
        slot[:, cols] = (dot(scores[:, part], right, TN) * scale).astype(slot.dtype)


def put_local(term, term_ref, local_ref, export_ref, start_ref, cols):
    term_ref[...] = term
    local_ref[:, cols] = term.astype(local_ref.dtype)
    start = pl.multiple_of(start_ref[0], BLK)
    export_ref[:, cols] = term_ref[pl.ds(start, BLK)]


def grad_out_kernel(stat_ref, o_ref, grad_ref, gain_ref, p_ref, *refs):
    normed_ref, d_ref, terms_ref, inverse_ref, factor_ref = refs
    tokens = o_ref.shape[0]
    stats = jnp.sum(stat_ref[...], axis=0)
    squares = jnp.broadcast_to(stats[0:1], (HEAD_SIZE, tokens)).T
    cross = jnp.broadcast_to(stats[1:2], (HEAD_SIZE, tokens)).T
    inverse = lax.rsqrt(squares / FEAT + epsilon)
    inverse_ref[...] = inverse
    factor_ref[...] = inverse * inverse * inverse * cross / FEAT

    @pl.loop(0, p_ref.shape[0])
    def _(h):
        cols = head_columns(h)
        out = o_ref[:, cols]
        inverse = inverse_ref[...]
        gain = gain_ref[:, cols]
        scaled = grad_ref[:, cols].astype(jnp.float32) * gain
        normed_ref[:, cols] = (out * inverse * gain).astype(normed_ref.dtype)
        d_attended = (inverse * scaled - out * factor_ref[...]).astype(d_ref.dtype)
        d_ref[:, cols] = d_attended
        terms_ref[:, cols] = dot(p_ref[h], d_attended, TN).astype(terms_ref.dtype)


def score_rows(d_ref, o_ref, value_cat, p_ref, h, rows, cols):
    d_attended = d_ref[rows, cols]
    delta = jnp.sum(d_attended.astype(jnp.float32) * o_ref[rows, cols], axis=1, keepdims=True)
    dprob = dot(d_attended, value_cat[...], NT)
    return (p_ref[h, rows].astype(jnp.float32) * (dprob - delta)).astype(jnp.bfloat16)


def middle_kernel(nblocks, n, start_ref, q_ref, o_ref, d_ref, pa_ref, pb_ref, *refs):
    key_in, value_in = refs[:n], refs[n : 2 * n]
    local_ref, export_ref, dq_ref, terms_ref = refs[2 * n : 2 * n + 4]
    slots = refs[2 * n + 4 : -4]
    key_cat, value_cat, score_ref, term_ref = refs[-4:]
    tokens = d_ref.shape[0]

    @pl.loop(0, pa_ref.shape[0])
    def _(h):
        cols = head_columns(h)
        gather_rows(key_cat, key_in, cols)
        gather_rows(value_cat, value_in, cols)
        put_terms(pa_ref[h], d_ref[:, cols], slots, tokens, cols, 1.0)
        term = dot(pa_ref[h, :, :tokens], d_ref[:, cols], TN)
        put_local(term, term_ref, local_ref, export_ref, start_ref, cols)
        for g in range(nblocks):
            rows = slice(g * BLK, (g + 1) * BLK)
            dscore = score_rows(d_ref, o_ref, value_cat, pb_ref, h, rows, cols)
            score_ref[rows] = dscore
            dq_ref[rows, cols] = dot(dscore, key_cat[...], NN)
        term = dot(score_ref[...], q_ref[:, cols], TN) * softmax_scale
        terms_ref[:, cols] = term.astype(terms_ref.dtype)


def key_kernel(nblocks, start_ref, q_ref, o_ref, d_ref, p_ref, dq_in, *refs):
    n = (len(refs) - 6) // 3
    key_cat, value_cat, score_ref, term_ref = refs[-4:]
    dq_ref, local_ref, export_ref = refs[2 * n : 2 * n + 3]
    slots = refs[2 * n + 3 : -4]
    tokens = q_ref.shape[0]

    @pl.loop(0, p_ref.shape[0])
    def _(h):
        cols = head_columns(h)
        gather_rows(key_cat, refs[:n], cols)
        gather_rows(value_cat, refs[n : 2 * n], cols)
        for g in range(nblocks):
            rows = slice(g * BLK, (g + 1) * BLK)
            dscore = score_rows(d_ref, o_ref, value_cat, p_ref, h, rows, cols)
            score_ref[rows] = dscore
            dq = dq_in[rows, cols] + dot(dscore, key_cat[...], NN)
            dq_ref[rows, cols] = (dq * softmax_scale).astype(dq_ref.dtype)
        put_terms(score_ref, q_ref[:, cols], slots, tokens, cols, softmax_scale)
        term = dot(score_ref[:, :tokens], q_ref[:, cols], TN) * softmax_scale
        put_local(term, term_ref, local_ref, export_ref, start_ref, cols)


def after(x, *earlier):
    return lax.optimization_barrier((x, earlier))[0]


def shards(queries, keys, values, gain, grad_out, pattern):
    n_seq = lax.axis_size("seq")
    far = n_seq // 2
    myself = lax.axis_index("seq")
    tokens, width = queries.shape
    heads = width // HEAD_SIZE
    nblocks = tokens // BLK
    a, b = myself // 2, myself % 2
    bf16, f32 = jnp.bfloat16, jnp.float32

    def move(x, to, among=None):
        among = range(far) if among is None else among
        return lax.ppermute(x, "seq", [(i * 2 + j, to(i) * 2 + j) for i in among for j in range(2)])

    def swap(x):
        return lax.ppermute(x, "seq", [(i, i ^ 1) for i in range(n_seq)])

    ranges = jnp.stack(
        [myself]
        + [(a ^ k) * 2 + b for k in range(1, far)]
        + [(a ^ k) * 2 + 1 - b for k in range(far)]
    )

    smem = pl.BlockSpec(memory_space=pltpu.SMEM)
    vmem = pl.BlockSpec(memory_space=pltpu.VMEM)
    shape = jax.ShapeDtypeStruct

    def call(name, kernel, inputs, out_shape, scratch=(), in_smem=(), out_smem=(), limit=10):
        single = not isinstance(out_shape, list)
        n_out = 1 if single else len(out_shape)
        out_specs = [smem if i in out_smem else vmem for i in range(n_out)]
        return pl.pallas_call(
            kernel,
            in_specs=[smem if i in in_smem else vmem for i in range(len(inputs))],
            out_specs=out_specs[0] if single else out_specs,
            out_shape=out_shape,
            scratch_shapes=[pltpu.VMEM(*s) for s in scratch],
            compiler_params=pltpu.CompilerParams(vmem_limit_bytes=limit * 1024 * 1024),
            cost_estimate=pl.CostEstimate(flops=10**11, bytes_accessed=10**8, transcendentals=0),
            name=name,
        )(*inputs)

    slot_shape = shape((BLK, width), bf16)
    key_own, value_own, both_own, start_vec = call(
        "pick",
        functools.partial(pick_kernel, nblocks),
        [myself.reshape(1), pattern, keys, values],
        [slot_shape, slot_shape, shape((2 * BLK, width), bf16), shape((1,), jnp.int32)],
        in_smem=(0,),
        out_smem=(3,),
    )
    start = start_vec[0]

    n_first, n_rest = far, far - 1
    first = tokens + n_first * BLK
    rest = n_rest * BLK

    def probabilities(key_near, key_mates):
        return call(
            "softmax",
            functools.partial(softmax_kernel, nblocks, first),
            [ranges, pattern, queries, keys, *key_near, *key_mates],
            [shape((heads, tokens, first), bf16), shape((heads, tokens, rest), bf16)],
            [((first + rest, HEAD_SIZE), bf16)],
            in_smem=(0, 1),
        )

    if far == 4:
        inner, outer = (1, 2), (0, 3)
        is_inner = (a == 1) | (a == 2)

        both = swap(both_own)
        k0, v0 = both[:BLK], both[BLK:]
        k1 = move(key_own, lambda i: i ^ 1)
        k2 = move(key_own, lambda i: i ^ 2)
        km = move(key_own, lambda i: i ^ 3, inner)
        kf = move(k2, lambda i: i ^ 1, inner)
        v1 = move(after(value_own, k1), lambda i: i ^ 1)
        v2 = move(after(value_own, k2), lambda i: i ^ 2)
        m1 = swap(k1)
        m2 = swap(after(k2, both))
        vm = move(after(value_own, km), lambda i: i ^ 3, inner)
        k3 = jnp.where(is_inner, after(km, m1), kf)
        m3 = swap(k3)
        n1 = swap(after(v1, m2))
        vf = move(v2, lambda i: i ^ 1, inner)
        n2 = swap(after(v2, m3))
        v3 = jnp.where(is_inner, vm, vf)
        n3 = swap(after(v3, n1))
        key_near, key_mates = [k1, k2, k3], [k0, m1, m2, m3]
        value_near, value_mates = [v1, v2, v3], [v0, n1, n2, n3]
        prob_first, prob_rest = probabilities(key_near, key_mates)
    else:
        key_near = [move(key_own, lambda i, k=k: i ^ k) for k in range(1, far)]
        value_near = [move(value_own, lambda i, k=k: i ^ k) for k in range(1, far)]
        key_mates = [swap(x) for x in [key_own] + key_near]
        value_mates = [swap(x) for x in [value_own] + value_near]
        prob_first, prob_rest = probabilities(key_near, key_mates)

    gain_row = gain.reshape(1, width)
    local_shapes = [shape((tokens, width), bf16), shape((BLK, width), f32)]

    attended = call(
        "attend",
        attend_kernel,
        [prob_first, values, *value_near, value_mates[0]],
        shape((tokens, width), f32),
        [((first, HEAD_SIZE), bf16)],
    )

    attended, stats = call(
        "attend_rest",
        attend_rest_kernel,
        [prob_rest, attended, grad_out, gain_row, *value_mates[1:]],
        [shape((tokens, width), f32), shape((8, tokens), f32)],
        [((rest, HEAD_SIZE), bf16), ((tokens, HEAD_SIZE), f32), ((tokens, HEAD_SIZE), f32)],
    )

    stats = lax.all_gather(stats, "head")

    normed, d_attended, value_rest = call(
        "grad_out",
        grad_out_kernel,
        [stats, attended, grad_out, gain_row, prob_rest],
        [shape((tokens, width), bf16)] * 2 + [shape((rest, width), bf16)],
        [((tokens, HEAD_SIZE), f32)] * 2,
    )
    value_rest = swap(value_rest)

    value_local, value_mine, dq_rest, key_rest, *value_first = call(
        "middle",
        functools.partial(middle_kernel, nblocks, n_rest),
        [
            start_vec,
            queries,
            attended,
            d_attended,
            prob_first,
            prob_rest,
            *key_mates[1:],
            *value_mates[1:],
        ],
        local_shapes
        + [shape((tokens, width), f32), shape((rest, width), bf16)]
        + [slot_shape] * n_first,
        [
            ((rest, HEAD_SIZE), bf16),
            ((rest, HEAD_SIZE), bf16),
            ((tokens, rest), bf16),
            ((tokens, HEAD_SIZE), f32),
        ],
        in_smem=(0,),
    )
    key_rest = swap(key_rest)

    grad_queries, key_local, key_mine, *key_first = call(
        "key_terms",
        functools.partial(key_kernel, nblocks),
        [
            start_vec,
            queries,
            attended,
            d_attended,
            prob_first,
            dq_rest,
            keys,
            *key_near,
            key_mates[0],
            values,
            *value_near,
            value_mates[0],
        ],
        [shape((tokens, width), bf16)] + local_shapes + [slot_shape] * n_first,
        [((first, HEAD_SIZE), bf16)] * 2 + [((tokens, first), bf16), ((tokens, HEAD_SIZE), f32)],
        in_smem=(0,),
    )

    def add(*terms):
        return sum(t.astype(f32) for t in terms)

    def send_back(near, mate, rest, mine):
        rest = [rest[k * BLK : (k + 1) * BLK] for k in range(n_rest)]
        if far == 4:
            c3 = add(near[2], rest[2]).astype(bf16)
            forwarded = move(c3, lambda i: i ^ 1, outer)
            came3 = move(c3, lambda i: i ^ 3, inner)
            c2 = add(near[1], rest[1], forwarded).astype(bf16)
            came2 = move(c2, lambda i: i ^ 2)
            c1 = add(near[0], rest[0]).astype(bf16)
            came1 = move(c1, lambda i: i ^ 1)
            came = [came1, came2, came3]
        else:
            came = [
                move(add(near[k - 1], rest[k - 1]).astype(bf16), lambda i, k=k: i ^ k)
                for k in range(1, far)
            ]
        return add(mine, swap(mate), *came).astype(bf16)

    grad_values = lax.dynamic_update_slice_in_dim(
        value_local,
        send_back(value_first[: far - 1], value_first[far - 1], value_rest, value_mine),
        start,
        0,
    )
    grad_keys = lax.dynamic_update_slice_in_dim(
        key_local,
        send_back(key_first[: far - 1], key_first[far - 1], key_rest, key_mine),
        start,
        0,
    )
    return normed, grad_queries, grad_keys, grad_values


def solution(mesh):
    split = P("seq", "head")
    return jax.shard_map(
        shards,
        mesh=mesh,
        in_specs=(split, split, split, P("head"), split, P()),
        out_specs=(split, split, split, split),
        check_vma=False,
    )
```

```python
import functools

import jax
import jax.numpy as jnp
from jax import lax
from jax.experimental import pallas as pl
from jax.experimental.pallas import tpu as pltpu
from jax.sharding import PartitionSpec as P

HEAD_SIZE = 128
BLK = 128
LOC = 3
REM = 7
FEAT = 4096
LOW = -1e30

epsilon = 1e-06
softmax_scale = 1.0 / HEAD_SIZE**0.5

NT = (((1,), (1,)), ((), ()))
NN = (((1,), (0,)), ((), ()))
TN = (((0,), (0,)), ((), ()))


def dot(a, b, dims):
    return lax.dot_general(a, b, dims, preferred_element_type=jnp.float32)


def head_columns(h):
    return pl.ds(pl.multiple_of(h * HEAD_SIZE, HEAD_SIZE), HEAD_SIZE)


def blocks(first, count=1):
    return slice(first * BLK, (first + count) * BLK)


def pick_kernel(
    nblocks, me_ref, pattern_hbm, key_hbm, value_hbm, own_ref, start_ref, pattern_ref, key_ref, value_ref, sems
):
    copies = [
        pltpu.make_async_copy(source, target, sems.at[i])
        for i, (source, target) in enumerate(
            [(pattern_hbm, pattern_ref), (key_hbm, key_ref), (value_hbm, value_ref)]
        )
    ]
    for copy in copies:
        copy.start()
    copies[0].wait()
    pattern = pattern_ref[...]
    low = me_ref[0] * nblocks
    row = lax.broadcasted_iota(jnp.int32, pattern.shape, 1)
    inside = (pattern >= low) & (pattern < low + nblocks)
    others = (row < low) | (row >= low + nblocks)
    offset = jnp.where(inside & others, pattern - low, 0).astype(jnp.float32)
    start = pl.multiple_of(jnp.max(offset).astype(jnp.int32) * BLK, BLK)
    start_ref[0] = start
    copies[1].wait()
    copies[2].wait()
    own_ref[:BLK] = key_ref[pl.ds(start, BLK)]
    own_ref[BLK:] = value_ref[pl.ds(start, BLK)]


def gather_rows(cat_ref, pieces, cols):
    at = 0
    for piece, rows in pieces:
        size = rows.stop - rows.start
        cat_ref[at : at + size] = piece[rows, cols]
        at += size


def keys_of(slots):
    return [(slot, blocks(0)) for slot in slots]


def values_of(slots):
    return [(slot, blocks(1)) for slot in slots]


def is_listed(nblocks, ranges_ref, pattern_ref, g, local=None, place=None):
    low = ranges_ref[0] * nblocks
    listed = None
    for i in range(LOC) if place is None else range(LOC, LOC + REM):
        entry = pattern_ref[i, low + g]
        same = entry == low + local if place is None else entry // nblocks == ranges_ref[place]
        listed = same if listed is None else listed | same
    return jnp.where(listed, 0.0, LOW)


def biased(scores, biases):
    parts = [scores[:, blocks(j)] for j in range(len(biases))]
    parts = [p if bias is None else p + bias for p, bias in zip(parts, biases)]
    return jnp.concatenate(parts, axis=1)


def first_scores_kernel(nblocks, far_bias, ranges_ref, pattern_ref, q_ref, k_ref, *refs):
    slots = refs[:-4]
    p_ref, peak_ref, total_ref, cat_ref = refs[-4:]
    listed = functools.partial(is_listed, nblocks, ranges_ref, pattern_ref)
    biases = [
        [listed(g, local=j) for j in range(nblocks)]
        + [listed(g, place=1 + j) if far_bias else None for j in range(len(slots))]
        for g in range(nblocks)
    ]

    @pl.loop(0, p_ref.shape[0])
    def _(h):
        cols = head_columns(h)
        gather_rows(cat_ref, [(k_ref, blocks(0, nblocks))] + keys_of(slots), cols)
        for g in range(nblocks):
            rows = blocks(g)
            scores = dot(q_ref[rows, cols], cat_ref[...], NT) * softmax_scale
            scores = biased(scores, biases[g])
            peak = jnp.max(scores, axis=1, keepdims=True)
            expo = jnp.exp(scores - peak)
            total = jnp.sum(expo, axis=1, keepdims=True)
            p_ref[h, rows] = expo.astype(p_ref.dtype)
            peak_ref[h, rows] = jnp.broadcast_to(peak, (BLK, HEAD_SIZE))
            total_ref[h, rows] = jnp.broadcast_to(total, (BLK, HEAD_SIZE))


def first_attend_kernel(nblocks, p_ref, v_ref, *refs):
    slots = refs[:-2]
    o_ref, cat_ref = refs[-2:]

    @pl.loop(0, p_ref.shape[0])
    def _(h):
        cols = head_columns(h)
        gather_rows(cat_ref, [(v_ref, blocks(0, nblocks))] + values_of(slots), cols)
        o_ref[:, cols] = dot(p_ref[h], cat_ref[...], NN)


def second_kernel(
    nblocks,
    far_bias,
    n_first,
    ranges_ref,
    pattern_ref,
    q_ref,
    peak_ref,
    total_ref,
    o_in,
    grad_ref,
    gain_ref,
    *refs,
):
    slots = refs[:-8]
    p_ref, scale_ref, o_ref, stat_ref, key_cat, value_cat, square_ref, cross_ref = refs[-8:]
    listed = functools.partial(is_listed, nblocks, ranges_ref, pattern_ref)
    biases = [
        [listed(g, place=1 + n_first + j) if far_bias else None for j in range(len(slots))]
        for g in range(nblocks)
    ]
    square_ref[...] = jnp.zeros_like(square_ref)
    cross_ref[...] = jnp.zeros_like(cross_ref)

    @pl.loop(0, p_ref.shape[0])
    def _(h):
        cols = head_columns(h)
        gather_rows(key_cat, keys_of(slots), cols)
        gather_rows(value_cat, values_of(slots), cols)
        scores = dot(q_ref[:, cols], key_cat[...], NT) * softmax_scale
        if far_bias:
            parts = [biased(scores[blocks(g)], biases[g]) for g in range(nblocks)]
            scores = jnp.concatenate(parts, axis=0)
        old = peak_ref[h]
        peak = jnp.maximum(old, jnp.max(scores, axis=1, keepdims=True))
        shrink = jnp.exp(old - peak)
        expo = jnp.exp(scores - jnp.concatenate([peak] * len(slots), axis=1))
        total = total_ref[h] * shrink + jnp.sum(expo, axis=1, keepdims=True)
        inverse = 1.0 / total
        prob = (expo * jnp.concatenate([inverse] * len(slots), axis=1)).astype(p_ref.dtype)
        p_ref[h] = prob
        scale = shrink * inverse
        scale_ref[h] = scale
        out = o_in[:, cols] * scale + dot(prob, value_cat[...], NN)
        o_ref[:, cols] = out
        scaled = grad_ref[:, cols].astype(jnp.float32) * gain_ref[:, cols]
        square_ref[...] += out * out
        cross_ref[...] += scaled * out

    stat_ref[0:1] = jnp.sum(square_ref[...].T, axis=0, keepdims=True)
    stat_ref[1:2] = jnp.sum(cross_ref[...].T, axis=0, keepdims=True)
    stat_ref[2:] = jnp.zeros_like(stat_ref[2:])


def score_grad(d, delta, scale, value_cat, parts):
    dprob = dot(d, value_cat, NT)
    result = []
    for j, (prob, takes) in enumerate(parts):
        part = prob.astype(jnp.float32) * (dprob[:, blocks(j)] - delta)
        result.append((part * scale if takes else part).astype(jnp.bfloat16))
    return jnp.concatenate(result, axis=1)


def put_slots(slots, prob_parts, d, d_scaled, dscore, q, cols):
    for j, (slot, (prob, takes)) in enumerate(zip(slots, prob_parts)):
        key_term = dot(dscore[:, blocks(j)], q, TN) * softmax_scale
        slot[:BLK, cols] = key_term.astype(slot.dtype)
        slot[BLK:, cols] = dot(prob, d_scaled if takes else d, TN).astype(slot.dtype)


def take(places, pa_ref, pb_ref, h):
    return [
        (pb_ref[h, :, blocks(j)], False) if part else (pa_ref[h, :, blocks(j)], True)
        for part, j in places
    ]


def grad_out_kernel(
    places,
    q_ref,
    stat_ref,
    o_ref,
    grad_ref,
    gain_ref,
    scale_ref,
    pa_ref,
    pb_ref,
    *refs,
):
    n = len(places)
    normed_ref, d_ref, scaled_d_ref, delta_ref, dq_ref = refs[n : n + 5]
    outs = refs[n + 5 : 2 * n + 5]
    inverse_ref, factor_ref, key_cat, value_cat = refs[2 * n + 5 :]
    tokens = o_ref.shape[0]
    stats = jnp.sum(stat_ref[...], axis=0)
    squares = jnp.broadcast_to(stats[0:1], (HEAD_SIZE, tokens)).T
    cross = jnp.broadcast_to(stats[1:2], (HEAD_SIZE, tokens)).T
    inverse = lax.rsqrt(squares / FEAT + epsilon)
    inverse_ref[...] = inverse
    factor_ref[...] = inverse * inverse * inverse * cross / FEAT

    @pl.loop(0, pa_ref.shape[0])
    def _(h):
        cols = head_columns(h)
        gather_rows(key_cat, keys_of(refs[:n]), cols)
        gather_rows(value_cat, values_of(refs[:n]), cols)
        out = o_ref[:, cols]
        inverse = inverse_ref[...]
        gain = gain_ref[:, cols]
        scaled = grad_ref[:, cols].astype(jnp.float32) * gain
        normed_ref[:, cols] = (out * inverse * gain).astype(normed_ref.dtype)
        d_attended = inverse * scaled - out * factor_ref[...]
        d = d_attended.astype(d_ref.dtype)
        d_scaled = (d_attended * scale_ref[h]).astype(d_ref.dtype)
        d_ref[:, cols] = d
        scaled_d_ref[:, cols] = d_scaled
        delta = jnp.sum(d.astype(jnp.float32) * out, axis=1, keepdims=True)
        delta = jnp.broadcast_to(delta, out.shape)
        delta_ref[h] = delta
        parts = take(places, pa_ref, pb_ref, h)
        dscore = score_grad(d, delta, scale_ref[h], value_cat[...], parts)
        dq_ref[:, cols] = dot(dscore, key_cat[...], NN)
        put_slots(outs, parts, d, d_scaled, dscore, q_ref[:, cols], cols)


def slots_kernel(places, q_ref, d_ref, scaled_d_ref, delta_ref, scale_ref, pa_ref, pb_ref, dq_in, *refs):
    n = len(places)
    dq_ref = refs[n]
    outs = refs[n + 1 : 2 * n + 1]
    key_cat, value_cat = refs[2 * n + 1 :]

    @pl.loop(0, pa_ref.shape[0])
    def _(h):
        cols = head_columns(h)
        gather_rows(key_cat, keys_of(refs[:n]), cols)
        gather_rows(value_cat, values_of(refs[:n]), cols)
        parts = take(places, pa_ref, pb_ref, h)
        d = d_ref[:, cols]
        dscore = score_grad(d, delta_ref[h], scale_ref[h], value_cat[...], parts)
        dq_ref[:, cols] = dq_in[:, cols] + dot(dscore, key_cat[...], NN)
        put_slots(outs, parts, d, scaled_d_ref[:, cols], dscore, q_ref[:, cols], cols)


def local_kernel(
    nblocks,
    start_ref,
    q_ref,
    k_ref,
    v_ref,
    d_ref,
    scaled_d_ref,
    delta_ref,
    scale_ref,
    pa_ref,
    dq_in,
    dq_ref,
    key_local_ref,
    value_local_ref,
    export_ref,
    key_term,
    value_term,
):
    start = pl.multiple_of(start_ref[0], BLK)
    tokens = q_ref.shape[0]

    @pl.loop(0, pa_ref.shape[0])
    def _(h):
        cols = head_columns(h)
        parts = [(pa_ref[h, :, blocks(j)], True) for j in range(nblocks)]
        dscore = score_grad(d_ref[:, cols], delta_ref[h], scale_ref[h], v_ref[:, cols], parts)
        dq = dq_in[:, cols] + dot(dscore, k_ref[:, cols], NN)
        dq_ref[:, cols] = (dq * softmax_scale).astype(dq_ref.dtype)
        key_term[...] = dot(dscore, q_ref[:, cols], TN) * softmax_scale
        value_term[...] = dot(pa_ref[h, :, :tokens], scaled_d_ref[:, cols], TN)
        key_local_ref[:, cols] = key_term[...].astype(key_local_ref.dtype)
        value_local_ref[:, cols] = value_term[...].astype(value_local_ref.dtype)
        export_ref[:BLK, cols] = key_term[pl.ds(start, BLK)]
        export_ref[BLK:, cols] = value_term[pl.ds(start, BLK)]


def finish_kernel(start_ref, mine_ref, *refs):
    came = refs[:-4]
    key_out, value_out = refs[-2:]
    total = mine_ref[...]
    for term in came:
        total = total + term[...].astype(jnp.float32)
    key_out[...] = total[:BLK].astype(key_out.dtype)
    value_out[...] = total[BLK:].astype(value_out.dtype)


def after(x, *earlier):
    return lax.optimization_barrier((x, earlier))[0]


def shards(queries, keys, values, gain, grad_out, pattern):
    n_seq = lax.axis_size("seq")
    far = n_seq // 2
    myself = lax.axis_index("seq")
    tokens, width = queries.shape
    heads = width // HEAD_SIZE
    nblocks = tokens // BLK
    a, b = myself // 2, myself % 2
    bf16, f32 = jnp.bfloat16, jnp.float32
    pattern = pattern.T
    inner, outer = (1, 2), (0, 3)

    def move(x, to, among=None):
        among = range(far) if among is None else among
        return lax.ppermute(x, "seq", [(i * 2 + j, to(i) * 2 + j) for i in among for j in range(2)])

    def swap(x):
        return lax.ppermute(x, "seq", [(i, i ^ 1) for i in range(n_seq)])

    half = far // 2
    is_inner = (a == 1) | (a == 2)
    sources = [a ^ k for k in range(1, far)]
    if far == 4:
        sources[1:] = [jnp.where(is_inner, a ^ 3, a ^ 2), jnp.where(is_inner, a ^ 2, a ^ 3)]
    near_ranges = [s * 2 + b for s in sources]
    mate_ranges = [s * 2 + 1 - b for s in [a] + sources]
    ranges = jnp.stack(
        [myself] + near_ranges[:-1] + mate_ranges[:half] + near_ranges[-1:] + mate_ranges[half:]
    )
    far_bias = n_seq - 1 != REM

    smem = pl.BlockSpec(memory_space=pltpu.SMEM)
    vmem = pl.BlockSpec(memory_space=pltpu.VMEM)
    shape = jax.ShapeDtypeStruct

    def call(name, kernel, inputs, out_shape, scratch=(), in_smem=(), out_smem=(), cost=10**8):
        single = not isinstance(out_shape, list)
        n_out = 1 if single else len(out_shape)
        out_specs = [smem if i in out_smem else vmem for i in range(n_out)]
        return pl.pallas_call(
            kernel,
            in_specs=[smem if i in in_smem else vmem for i in range(len(inputs))],
            out_specs=out_specs[0] if single else out_specs,
            out_shape=out_shape,
            scratch_shapes=[pltpu.VMEM(*s) for s in scratch],
            compiler_params=pltpu.CompilerParams(vmem_limit_bytes=12 * 1024 * 1024),
            cost_estimate=pl.CostEstimate(flops=cost * 1000, bytes_accessed=cost, transcendentals=0),
            name=name,
        )(*inputs)

    hbm = pl.BlockSpec(memory_space=pltpu.MemorySpace.HBM)
    own, start_vec = pl.pallas_call(
        functools.partial(pick_kernel, nblocks),
        in_specs=[smem, hbm, hbm, hbm],
        out_specs=[vmem, smem],
        out_shape=[shape((2 * BLK, width), bf16), shape((1,), jnp.int32)],
        scratch_shapes=[
            pltpu.VMEM(pattern.shape, jnp.int32),
            pltpu.VMEM((tokens, width), bf16),
            pltpu.VMEM((tokens, width), bf16),
            pltpu.SemaphoreType.DMA((3,)),
        ],
        name="pick",
    )(myself.reshape(1), pattern, keys, values)

    if far == 4:
        m0 = swap(own)
        s1 = move(own, lambda i: i ^ 1)
        mid1 = move(own, lambda i: i ^ 3, inner)
        m1 = swap(after(s1, m0))
        mid2 = move(s1, lambda i: i ^ 3, inner)
        end2 = move(mid1, lambda i: i ^ 1, inner)
        s2 = jnp.where(is_inner, mid1, end2)
        m2 = swap(after(s2, m1))
        end3 = move(mid2, lambda i: i ^ 1, inner)
        s3 = jnp.where(is_inner, mid2, end3)
        m3 = swap(after(s3, m2))
        near, mates = [s1, s2, s3], [m0, m1, m2, m3]
    else:
        near = [move(own, lambda i, k=k: i ^ k) for k in range(1, far)]
        mates = [swap(x) for x in [own] + near]
    slots_a = near[:-1] + mates[:half]
    slots_b = near[-1:] + mates[half:]
    cols_a = tokens + len(slots_a) * BLK
    cols_b = len(slots_b) * BLK
    gain_row = gain.reshape(1, width)
    rows_shape = shape((heads, tokens, HEAD_SIZE), f32)
    wide16, wide32 = shape((tokens, width), bf16), shape((tokens, width), f32)

    prob_a, peak_a, total_a = call(
        "first_scores",
        functools.partial(first_scores_kernel, nblocks, far_bias),
        [ranges, pattern, queries, keys, *slots_a],
        [shape((heads, tokens, cols_a), bf16), rows_shape, rows_shape],
        [((cols_a, HEAD_SIZE), bf16)],
        in_smem=(0, 1),
    )
    attended = call(
        "first_attend",
        functools.partial(first_attend_kernel, nblocks),
        [prob_a, values, *slots_a],
        wide32,
        [((cols_a, HEAD_SIZE), bf16)],
    )
    prob_b, scale_a, attended, stats = call(
        "second",
        functools.partial(second_kernel, nblocks, far_bias, len(slots_a)),
        [ranges, pattern, queries, peak_a, total_a, attended, grad_out, gain_row, *slots_b],
        [shape((heads, tokens, cols_b), bf16), rows_shape, wide32, shape((8, tokens), f32)],
        [((cols_b, HEAD_SIZE), bf16)] * 2 + [((tokens, HEAD_SIZE), f32)] * 2,
        in_smem=(0, 1),
    )

    stats = lax.all_gather(stats, "head")

    near_places = [(0, nblocks + k) for k in range(far - 2)] + [(1, 0)]
    mate_places = [(0, nblocks + far - 2 + k) for k in range(half)]
    mate_places += [(1, 1 + k) for k in range(far - half)]
    pair = shape((2 * BLK, width), bf16)

    def cats(n):
        return [((n * BLK, HEAD_SIZE), bf16)] * 2

    normed, d_attended, d_scaled, delta, dq, mate_last = call(
        "grad_out",
        functools.partial(grad_out_kernel, mate_places[-1:]),
        [queries, stats, attended, grad_out, gain_row, scale_a, prob_a, prob_b, mates[-1]],
        [wide16, wide16, wide16, rows_shape, wide32, pair],
        [((tokens, HEAD_SIZE), f32)] * 2 + cats(1),
    )

    def slot_terms(name, places, slots, dq):
        n = len(slots)
        return call(
            name,
            functools.partial(slots_kernel, places),
            [queries, d_attended, d_scaled, delta, scale_a, prob_a, prob_b, dq, *slots],
            [wide32] + [pair] * n,
            cats(n),
        )

    def add(*terms):
        return sum(t.astype(f32) for t in terms).astype(bf16)

    y_last = swap(mate_last)
    if far == 4:
        dq, mate2, mate1, near3, near2 = slot_terms(
            "terms_far",
            [mate_places[2], mate_places[1], near_places[2], near_places[1]],
            [mates[2], mates[1], near[2], near[1]],
            dq,
        )
        y2 = swap(mate2)
        y1 = swap(after(mate1, y_last))
        c3 = add(near3, y_last)
        end3 = move(c3, lambda i: i ^ 1, outer)
        dq, near1, mate0 = slot_terms(
            "terms_near", [near_places[0], mate_places[0]], [near[0], mates[0]], after(dq, c3)
        )
        mid3 = move(add(c3, end3), lambda i: i ^ 3, inner)
        c2 = add(after(near2, near1), y2)
        end2 = move(c2, lambda i: i ^ 1, outer)
        dq = after(dq, y2, end3)
    else:
        dq, mate0, near_last = slot_terms(
            "terms_ends",
            [mate_places[0], near_places[-1]],
            [mates[0], near[-1]],
            dq,
        )
        came = [swap(mate0), move(add(near_last, y_last), lambda i: i ^ (far - 1))]
        for k in range(1, far - 1):
            dq, mate_k, near_k = slot_terms(
                "terms",
                [mate_places[k], near_places[k - 1]],
                [mates[k], near[k - 1]],
                dq,
            )
            came.append(move(add(near_k, swap(mate_k)), lambda i, k=k: i ^ k))

    grad_queries, key_local, value_local, mine = call(
        "terms_local",
        functools.partial(local_kernel, nblocks),
        [start_vec, queries, keys, values, d_attended, d_scaled, delta, scale_a, prob_a, dq],
        [wide16, wide16, wide16, shape((2 * BLK, width), f32)],
        [((tokens, HEAD_SIZE), f32)] * 2,
        in_smem=(0,),
    )
    if far == 4:
        mid2 = move(add(c2, end2), lambda i: i ^ 3, inner)
        c1 = add(after(near1, mine), y1, mid3)
        y0 = swap(after(mate0, y1))
        came = [move(c1, lambda i: i ^ 1), mid2, y0]
    at = 2 + len(came)
    block = pl.BlockSpec((BLK, width), lambda i, place: (place[0], 0))
    grad_keys, grad_values = pl.pallas_call(
        finish_kernel,
        grid_spec=pltpu.PrefetchScalarGridSpec(
            num_scalar_prefetch=1,
            grid=(1,),
            in_specs=[vmem] * (1 + len(came)) + [hbm, hbm],
            out_specs=[block, block],
        ),
        out_shape=[wide16, wide16],
        input_output_aliases={at: 0, at + 1: 1},
        name="finish",
    )(start_vec // BLK, mine, *came, key_local, value_local)
    return normed, grad_queries, grad_keys, grad_values


def solution(mesh):
    split = P("seq", "head")
    return jax.shard_map(
        shards,
        mesh=mesh,
        in_specs=(split, split, split, P("head"), split, P()),
        out_specs=(split, split, split, split),
        check_vma=False,
    )
```

```python
import functools

import jax
import jax.numpy as jnp
from jax import lax
from jax.experimental import pallas as pl
from jax.experimental.pallas import tpu as pltpu
from jax.sharding import PartitionSpec as P

HEAD_SIZE = 128
BLK = 128
LOC = 3
REM = 7
FEAT = 4096
LOW = -1e30

epsilon = 1e-06
softmax_scale = 1.0 / HEAD_SIZE**0.5

NT = (((1,), (1,)), ((), ()))
NN = (((1,), (0,)), ((), ()))
TN = (((0,), (0,)), ((), ()))


def dot(a, b, dims):
    return lax.dot_general(a, b, dims, preferred_element_type=jnp.float32)


def head_columns(h):
    return pl.ds(pl.multiple_of(h * HEAD_SIZE, HEAD_SIZE), HEAD_SIZE)


def blocks(first, count=1):
    return slice(first * BLK, (first + count) * BLK)


def pick_kernel(
    nblocks, me_ref, pattern_hbm, key_hbm, value_hbm, own_ref, start_ref, pattern_ref, key_ref, value_ref, sems
):
    copies = [
        pltpu.make_async_copy(source, target, sems.at[i])
        for i, (source, target) in enumerate(
            [(pattern_hbm, pattern_ref), (key_hbm, key_ref), (value_hbm, value_ref)]
        )
    ]
    for copy in copies:
        copy.start()
    copies[0].wait()
    pattern = pattern_ref[...]
    low = me_ref[0] * nblocks
    row = lax.broadcasted_iota(jnp.int32, pattern.shape, 1)
    inside = (pattern >= low) & (pattern < low + nblocks)
    others = (row < low) | (row >= low + nblocks)
    offset = jnp.where(inside & others, pattern - low, 0).astype(jnp.float32)
    start = pl.multiple_of(jnp.max(offset).astype(jnp.int32) * BLK, BLK)
    start_ref[0] = start
    copies[1].wait()
    copies[2].wait()
    own_ref[:BLK] = key_ref[pl.ds(start, BLK)]
    own_ref[BLK:] = value_ref[pl.ds(start, BLK)]


def gather_rows(cat_ref, pieces, cols):
    at = 0
    for piece, rows in pieces:
        size = rows.stop - rows.start
        cat_ref[at : at + size] = piece[rows, cols]
        at += size


def keys_of(slots):
    return [(slot, blocks(0)) for slot in slots]


def values_of(slots):
    return [(slot, blocks(1)) for slot in slots]


def is_listed(nblocks, ranges_ref, pattern_ref, g, local=None, place=None):
    low = ranges_ref[0] * nblocks
    listed = None
    for i in range(LOC) if place is None else range(LOC, LOC + REM):
        entry = pattern_ref[i, low + g]
        same = entry == low + local if place is None else entry // nblocks == ranges_ref[place]
        listed = same if listed is None else listed | same
    return jnp.where(listed, 0.0, LOW)


def biased(scores, biases):
    parts = [scores[:, blocks(j)] for j in range(len(biases))]
    parts = [p if bias is None else p + bias for p, bias in zip(parts, biases)]
    return jnp.concatenate(parts, axis=1)


def first_scores_kernel(nblocks, far_bias, ranges_ref, pattern_ref, q_ref, k_ref, *refs):
    slots = refs[:-4]
    p_ref, peak_ref, total_ref, cat_ref = refs[-4:]
    listed = functools.partial(is_listed, nblocks, ranges_ref, pattern_ref)
    biases = [
        [listed(g, local=j) for j in range(nblocks)]
        + [listed(g, place=1 + j) if far_bias else None for j in range(len(slots))]
        for g in range(nblocks)
    ]

    @pl.loop(0, p_ref.shape[0], unroll=4)
    def _(h):
        cols = head_columns(h)
        gather_rows(cat_ref, [(k_ref, blocks(0, nblocks))] + keys_of(slots), cols)
        for g in range(nblocks):
            rows = blocks(g)
            scores = dot(q_ref[rows, cols], cat_ref[...], NT) * softmax_scale
            scores = biased(scores, biases[g])
            peak = jnp.max(scores, axis=1, keepdims=True)
            expo = jnp.exp(scores - peak)
            total = jnp.sum(expo, axis=1, keepdims=True)
            p_ref[h, rows] = expo.astype(p_ref.dtype)
            peak_ref[h, rows] = jnp.broadcast_to(peak, (BLK, HEAD_SIZE))
            total_ref[h, rows] = jnp.broadcast_to(total, (BLK, HEAD_SIZE))


def first_attend_kernel(nblocks, p_ref, v_ref, *refs):
    slots = refs[:-2]
    o_ref, cat_ref = refs[-2:]

    @pl.loop(0, p_ref.shape[0], unroll=4)
    def _(h):
        cols = head_columns(h)
        gather_rows(cat_ref, [(v_ref, blocks(0, nblocks))] + values_of(slots), cols)
        o_ref[:, cols] = dot(p_ref[h], cat_ref[...], NN)


def later_biases(nblocks, far_bias, at, count, ranges_ref, pattern_ref):
    if not far_bias:
        return None
    listed = functools.partial(is_listed, nblocks, ranges_ref, pattern_ref)
    return [[listed(g, place=at + j) for j in range(count)] for g in range(nblocks)]


def later_scores(q, keys, biases):
    scores = dot(q, keys, NT) * softmax_scale
    if biases is None:
        return scores
    parts = [biased(scores[blocks(g)], biases[g]) for g in range(len(biases))]
    return jnp.concatenate(parts, axis=0)


def wide(x, like):
    return x if like.shape == x.shape else jnp.concatenate([x] * (like.shape[1] // BLK), axis=1)


def second_kernel(nblocks, far_bias, at, ranges_ref, pattern_ref, q_ref, peak_in, total_in, o_in, *refs):
    slots = refs[:-7]
    p_ref, shrink_ref, peak_ref, total_ref, o_ref, key_cat, value_cat = refs[-7:]
    biases = later_biases(nblocks, far_bias, at, len(slots), ranges_ref, pattern_ref)

    @pl.loop(0, p_ref.shape[0], unroll=4)
    def _(h):
        cols = head_columns(h)
        gather_rows(key_cat, keys_of(slots), cols)
        gather_rows(value_cat, values_of(slots), cols)
        scores = later_scores(q_ref[:, cols], key_cat[...], biases)
        old = peak_in[h]
        peak = jnp.maximum(old, jnp.max(scores, axis=1, keepdims=True))
        shrink = jnp.exp(old - peak)
        expo = jnp.exp(scores - wide(peak, scores))
        expo16 = expo.astype(p_ref.dtype)
        p_ref[h] = expo16
        shrink_ref[h] = shrink
        peak_ref[h] = peak
        total_ref[h] = total_in[h] * shrink + jnp.sum(expo, axis=1, keepdims=True)
        o_ref[:, cols] = o_in[:, cols] * shrink + dot(expo16, value_cat[...], NN)


def third_kernel(
    nblocks,
    far_bias,
    at,
    ranges_ref,
    pattern_ref,
    q_ref,
    peak_ref,
    total_ref,
    shrink_ref,
    o_in,
    grad_ref,
    gain_ref,
    slot_ref,
    p_ref,
    scale_a_ref,
    scale_b_ref,
    o_ref,
    stat_ref,
    square_ref,
    cross_ref,
):
    biases = later_biases(nblocks, far_bias, at, 1, ranges_ref, pattern_ref)
    square_ref[...] = jnp.zeros_like(square_ref)
    cross_ref[...] = jnp.zeros_like(cross_ref)

    @pl.loop(0, p_ref.shape[0], unroll=True)
    def _(h):
        cols = head_columns(h)
        scores = later_scores(q_ref[:, cols], slot_ref[blocks(0), cols], biases)
        old = peak_ref[h]
        peak = jnp.maximum(old, jnp.max(scores, axis=1, keepdims=True))
        shrink = jnp.exp(old - peak)
        expo = jnp.exp(scores - peak)
        total = total_ref[h] * shrink + jnp.sum(expo, axis=1, keepdims=True)
        inverse = 1.0 / total
        prob = (expo * inverse).astype(p_ref.dtype)
        p_ref[h] = prob
        scale = shrink * inverse
        scale_b_ref[h] = scale
        scale_a_ref[h] = scale * shrink_ref[h]
        out = o_in[:, cols] * scale + dot(prob, slot_ref[blocks(1), cols], NN)
        o_ref[:, cols] = out
        scaled = grad_ref[:, cols].astype(jnp.float32) * gain_ref[:, cols]
        square_ref[...] += out * out
        cross_ref[...] += scaled * out

    squares = jnp.sum(square_ref[...].T, axis=0, keepdims=True)
    cross = jnp.sum(cross_ref[...].T, axis=0, keepdims=True)
    for g in range(nblocks):
        stat_ref[g : g + 1] = squares[:, blocks(g)]
        stat_ref[nblocks + g : nblocks + g + 1] = cross[:, blocks(g)]


def score_grad(d, delta, scales, value_cat, parts):
    dprob = dot(d, value_cat, NT)
    result = []
    for j, (prob, part) in enumerate(parts):
        term = prob.astype(jnp.float32) * (dprob[:, blocks(j)] - delta)
        term = term if scales[part] is None else term * scales[part]
        result.append(term.astype(jnp.bfloat16))
    return jnp.concatenate(result, axis=1)


def put_slots(slots, prob_parts, d_parts, dscore, q, cols):
    for j, (slot, (prob, part)) in enumerate(zip(slots, prob_parts)):
        key_term = dot(dscore[:, blocks(j)], q, TN) * softmax_scale
        slot[:BLK, cols] = key_term.astype(slot.dtype)
        slot[BLK:, cols] = dot(prob, d_parts[part], TN).astype(slot.dtype)


def take(places, p_refs, h):
    return [(p_refs[part][h, :, blocks(j)], part) for part, j in places]


def grad_out_kernel(
    place,
    q_ref,
    stat_ref,
    o_ref,
    grad_ref,
    gain_ref,
    scale_a_ref,
    scale_b_ref,
    p_ref,
    slot_ref,
    normed_ref,
    d_ref,
    d_a_ref,
    d_b_ref,
    delta_ref,
    dq_ref,
    out_ref,
    inverse_ref,
    factor_ref,
):
    tokens = o_ref.shape[0]
    stats = jnp.sum(stat_ref[...], axis=0)
    rows = [jnp.broadcast_to(stats[g : g + 1], (HEAD_SIZE, BLK)).T for g in range(stats.shape[0])]
    squares = jnp.concatenate(rows[: tokens // BLK], axis=0)
    cross = jnp.concatenate(rows[tokens // BLK :], axis=0)
    inverse = lax.rsqrt(squares / FEAT + epsilon)
    inverse_ref[...] = inverse
    factor_ref[...] = inverse * inverse * inverse * cross / FEAT

    @pl.loop(0, p_ref.shape[0], unroll=True)
    def _(h):
        cols = head_columns(h)
        out = o_ref[:, cols]
        inverse = inverse_ref[...]
        gain = gain_ref[:, cols]
        scaled = grad_ref[:, cols].astype(jnp.float32) * gain
        normed_ref[:, cols] = (out * inverse * gain).astype(normed_ref.dtype)
        d_attended = inverse * scaled - out * factor_ref[...]
        d = d_attended.astype(d_ref.dtype)
        d_ref[:, cols] = d
        d_a_ref[:, cols] = (d_attended * scale_a_ref[h]).astype(d_ref.dtype)
        d_b_ref[:, cols] = (d_attended * scale_b_ref[h]).astype(d_ref.dtype)
        delta = jnp.sum(d.astype(jnp.float32) * out, axis=1, keepdims=True)
        delta = jnp.broadcast_to(delta, out.shape)
        delta_ref[h] = delta
        parts = take([place], (None, None, p_ref), h)
        dscore = score_grad(d, delta, (None, None, None), slot_ref[blocks(1), cols], parts)
        dq_ref[:, cols] = dot(dscore, slot_ref[blocks(0), cols], NN)
        put_slots([out_ref], parts, (None, None, d), dscore, q_ref[:, cols], cols)


def slots_kernel(
    places, q_ref, d_ref, d_a_ref, d_b_ref, delta_ref, scale_a_ref, scale_b_ref, pa_ref, pb_ref, dq_in, *refs
):
    n = len(places)
    dq_ref = refs[n]
    outs = refs[n + 1 : 2 * n + 1]
    key_cat, value_cat = refs[2 * n + 1 :]

    @pl.loop(0, pa_ref.shape[0], unroll=4)
    def _(h):
        cols = head_columns(h)
        gather_rows(key_cat, keys_of(refs[:n]), cols)
        gather_rows(value_cat, values_of(refs[:n]), cols)
        parts = take(places, (pa_ref, pb_ref), h)
        scales = (scale_a_ref[h], scale_b_ref[h])
        dscore = score_grad(d_ref[:, cols], delta_ref[h], scales, value_cat[...], parts)
        dq_ref[:, cols] = dq_in[:, cols] + dot(dscore, key_cat[...], NN)
        put_slots(outs, parts, (d_a_ref[:, cols], d_b_ref[:, cols]), dscore, q_ref[:, cols], cols)


def local_kernel(
    nblocks,
    start_ref,
    q_ref,
    k_ref,
    v_ref,
    d_ref,
    scaled_d_ref,
    delta_ref,
    scale_ref,
    pa_ref,
    dq_in,
    dq_ref,
    key_local_ref,
    value_local_ref,
    export_ref,
    key_term,
    value_term,
):
    start = pl.multiple_of(start_ref[0], BLK)
    tokens = q_ref.shape[0]

    @pl.loop(0, pa_ref.shape[0], unroll=True)
    def _(h):
        cols = head_columns(h)
        parts = [(pa_ref[h, :, blocks(j)], 0) for j in range(nblocks)]
        dscore = score_grad(d_ref[:, cols], delta_ref[h], (scale_ref[h],), v_ref[:, cols], parts)
        dq = dq_in[:, cols] + dot(dscore, k_ref[:, cols], NN)
        dq_ref[:, cols] = (dq * softmax_scale).astype(dq_ref.dtype)
        key_term[...] = dot(dscore, q_ref[:, cols], TN) * softmax_scale
        value_term[...] = dot(pa_ref[h, :, :tokens], scaled_d_ref[:, cols], TN)
        key_local_ref[:, cols] = key_term[...].astype(key_local_ref.dtype)
        value_local_ref[:, cols] = value_term[...].astype(value_local_ref.dtype)
        export_ref[:BLK, cols] = key_term[pl.ds(start, BLK)]
        export_ref[BLK:, cols] = value_term[pl.ds(start, BLK)]


def finish_kernel(start_ref, mine_ref, *refs):
    came = refs[:-4]
    key_out, value_out = refs[-2:]
    total = mine_ref[...]
    for term in came:
        total = total + term[...].astype(jnp.float32)
    key_out[...] = total[:BLK].astype(key_out.dtype)
    value_out[...] = total[BLK:].astype(value_out.dtype)


def after(x, *earlier):
    return lax.optimization_barrier((x, earlier))[0]


def shards(queries, keys, values, gain, grad_out, pattern):
    n_seq = lax.axis_size("seq")
    far = n_seq // 2
    myself = lax.axis_index("seq")
    tokens, width = queries.shape
    heads = width // HEAD_SIZE
    nblocks = tokens // BLK
    a, b = myself // 2, myself % 2
    bf16, f32 = jnp.bfloat16, jnp.float32
    pattern = pattern.T
    inner, outer = (1, 2), (0, 3)

    def move(x, to, among=None):
        among = range(far) if among is None else among
        return lax.ppermute(x, "seq", [(i * 2 + j, to(i) * 2 + j) for i in among for j in range(2)])

    def swap(x):
        return lax.ppermute(x, "seq", [(i, i ^ 1) for i in range(n_seq)])

    half = far // 2
    is_inner = (a == 1) | (a == 2)
    sources = [a ^ k for k in range(1, far)]
    if far == 4:
        sources[1:] = [jnp.where(is_inner, a ^ 3, a ^ 2), jnp.where(is_inner, a ^ 2, a ^ 3)]
    near_ranges = [s * 2 + b for s in sources]
    mate_ranges = [s * 2 + 1 - b for s in [a] + sources]
    ranges = jnp.stack(
        [myself] + near_ranges[:-1] + mate_ranges[:half] + near_ranges[-1:] + mate_ranges[half:]
    )
    far_bias = n_seq - 1 != REM

    smem = pl.BlockSpec(memory_space=pltpu.SMEM)
    vmem = pl.BlockSpec(memory_space=pltpu.VMEM)
    shape = jax.ShapeDtypeStruct

    def call(name, kernel, inputs, out_shape, scratch=(), in_smem=(), out_smem=(), cost=10**8):
        single = not isinstance(out_shape, list)
        n_out = 1 if single else len(out_shape)
        out_specs = [smem if i in out_smem else vmem for i in range(n_out)]
        return pl.pallas_call(
            kernel,
            in_specs=[smem if i in in_smem else vmem for i in range(len(inputs))],
            out_specs=out_specs[0] if single else out_specs,
            out_shape=out_shape,
            scratch_shapes=[pltpu.VMEM(*s) for s in scratch],
            compiler_params=pltpu.CompilerParams(vmem_limit_bytes=12 * 1024 * 1024),
            cost_estimate=pl.CostEstimate(flops=cost * 1000, bytes_accessed=cost, transcendentals=0),
            name=name,
        )(*inputs)

    hbm = pl.BlockSpec(memory_space=pltpu.MemorySpace.HBM)
    own, start_vec = pl.pallas_call(
        functools.partial(pick_kernel, nblocks),
        in_specs=[smem, hbm, hbm, hbm],
        out_specs=[vmem, smem],
        out_shape=[shape((2 * BLK, width), bf16), shape((1,), jnp.int32)],
        scratch_shapes=[
            pltpu.VMEM(pattern.shape, jnp.int32),
            pltpu.VMEM((tokens, width), bf16),
            pltpu.VMEM((tokens, width), bf16),
            pltpu.SemaphoreType.DMA((3,)),
        ],
        name="pick",
    )(myself.reshape(1), pattern, keys, values)

    if far == 4:
        m0 = swap(own)
        s1 = move(own, lambda i: i ^ 1)
        mid1 = move(own, lambda i: i ^ 3, inner)
        m1 = swap(after(s1, m0))
        mid2 = move(s1, lambda i: i ^ 3, inner)
        end2 = move(mid1, lambda i: i ^ 1, inner)
        s2 = jnp.where(is_inner, mid1, end2)
        m2 = swap(after(s2, m1))
        end3 = move(mid2, lambda i: i ^ 1, inner)
        s3 = jnp.where(is_inner, mid2, end3)
        m3 = swap(after(s3, m2))
        near, mates = [s1, s2, s3], [m0, m1, m2, m3]
    else:
        near = [move(own, lambda i, k=k: i ^ k) for k in range(1, far)]
        mates = [swap(x) for x in [own] + near]
    slots_a = near[:-1] + mates[:half]
    slots_b = near[-1:] + mates[half:-1]
    cols_a = tokens + len(slots_a) * BLK
    cols_b = len(slots_b) * BLK
    gain_row = gain.reshape(1, width)
    rows_shape = shape((heads, tokens, HEAD_SIZE), f32)
    wide16, wide32 = shape((tokens, width), bf16), shape((tokens, width), f32)

    prob_a, peak_a, total_a = call(
        "first_scores",
        functools.partial(first_scores_kernel, nblocks, far_bias),
        [ranges, pattern, queries, keys, *slots_a],
        [shape((heads, tokens, cols_a), bf16), rows_shape, rows_shape],
        [((cols_a, HEAD_SIZE), bf16)],
        in_smem=(0, 1),
    )
    attended = call(
        "first_attend",
        functools.partial(first_attend_kernel, nblocks),
        [prob_a, values, *slots_a],
        wide32,
        [((cols_a, HEAD_SIZE), bf16)],
    )
    prob_b, shrink, peak_b, total_b, attended = call(
        "second",
        functools.partial(second_kernel, nblocks, far_bias, 1 + len(slots_a)),
        [ranges, pattern, queries, peak_a, total_a, attended, *slots_b],
        [shape((heads, tokens, cols_b), bf16), rows_shape, rows_shape, rows_shape, wide32],
        [((cols_b, HEAD_SIZE), bf16)] * 2,
        in_smem=(0, 1),
        cost=1000,
    )
    prob_c, scale_a, scale_b, attended, stats = call(
        "third",
        functools.partial(third_kernel, nblocks, far_bias, 1 + len(slots_a) + len(slots_b)),
        [ranges, pattern, queries, peak_b, total_b, shrink, attended, grad_out, gain_row, mates[-1]],
        [shape((heads, tokens, BLK), bf16), rows_shape, rows_shape, wide32, shape((2 * nblocks, BLK), f32)],
        [((tokens, HEAD_SIZE), f32)] * 2,
        in_smem=(0, 1),
    )

    stats = lax.all_gather(stats, "head")

    near_places = [(0, nblocks + k) for k in range(far - 2)] + [(1, 0)]
    mate_places = [(0, nblocks + far - 2 + k) for k in range(half)]
    mate_places += [(1, 1 + k) for k in range(far - half - 1)] + [(2, 0)]
    pair = shape((2 * BLK, width), bf16)

    def cats(n):
        return [((n * BLK, HEAD_SIZE), bf16)] * 2

    normed, d_attended, d_a, d_b, delta, dq, mate_last = call(
        "grad_out",
        functools.partial(grad_out_kernel, mate_places[-1]),
        [queries, stats, attended, grad_out, gain_row, scale_a, scale_b, prob_c, mates[-1]],
        [wide16, wide16, wide16, wide16, rows_shape, wide32, pair],
        [((tokens, HEAD_SIZE), f32)] * 2,
    )

    def slot_terms(name, places, slots, dq):
        n = len(slots)
        return call(
            name,
            functools.partial(slots_kernel, places),
            [queries, d_attended, d_a, d_b, delta, scale_a, scale_b, prob_a, prob_b, dq, *slots],
            [wide32] + [pair] * n,
            cats(n),
        )

    def add(*terms):
        return sum(t.astype(f32) for t in terms).astype(bf16)

    y_last = swap(mate_last)
    if far == 4:
        dq, mate2, mate1, near3, near2 = slot_terms(
            "terms_far",
            [mate_places[2], mate_places[1], near_places[2], near_places[1]],
            [mates[2], mates[1], near[2], near[1]],
            dq,
        )
        y2 = swap(mate2)
        y1 = swap(mate1)
        dq, near1, mate0 = slot_terms(
            "terms_near", [near_places[0], mate_places[0]], [near[0], mates[0]], dq
        )
        c3 = add(after(near3, near1), y_last)
        end3 = move(c3, lambda i: i ^ 1, outer)
        far3 = move(add(c3, end3), lambda i: i ^ 2, inner)
        dq = after(dq, c3)
    else:
        dq, mate0, near_last = slot_terms(
            "terms_ends",
            [mate_places[0], near_places[-1]],
            [mates[0], near[-1]],
            dq,
        )
        came = [swap(mate0), move(add(near_last, y_last), lambda i: i ^ (far - 1))]
        for k in range(1, far - 1):
            dq, mate_k, near_k = slot_terms(
                "terms",
                [mate_places[k], near_places[k - 1]],
                [mates[k], near[k - 1]],
                dq,
            )
            came.append(move(add(near_k, swap(mate_k)), lambda i, k=k: i ^ k))

    grad_queries, key_local, value_local, mine = call(
        "terms_local",
        functools.partial(local_kernel, nblocks),
        [start_vec, queries, keys, values, d_attended, d_a, delta, scale_a, prob_a, dq],
        [wide16, wide16, wide16, shape((2 * BLK, width), f32)],
        [((tokens, HEAD_SIZE), f32)] * 2,
        in_smem=(0,),
        cost=1000,
    )
    if far == 4:
        c2 = add(after(near2, mine), y2)
        end2 = move(c2, lambda i: i ^ 1, outer)
        c1 = add(near1, y1)
        near_came = move(c1, lambda i: i ^ 1)
        mid2 = move(add(c2, after(end2, far3)), lambda i: i ^ 3, inner)
        y0 = swap(after(mate0, y1))
        came = [far3, mid2, y0, near_came]
    at = 2 + len(came)
    block = pl.BlockSpec((BLK, width), lambda i, place: (place[0], 0))
    grad_keys, grad_values = pl.pallas_call(
        finish_kernel,
        grid_spec=pltpu.PrefetchScalarGridSpec(
            num_scalar_prefetch=1,
            grid=(1,),
            in_specs=[vmem] * (1 + len(came)) + [hbm, hbm],
            out_specs=[block, block],
        ),
        out_shape=[wide16, wide16],
        input_output_aliases={at: 0, at + 1: 1},
        name="finish",
    )(start_vec // BLK, mine, *came, key_local, value_local)
    return normed, grad_queries, grad_keys, grad_values


def solution(mesh):
    split = P("seq", "head")
    return jax.shard_map(
        shards,
        mesh=mesh,
        in_specs=(split, split, split, P("head"), split, P()),
        out_specs=(split, split, split, split),
        check_vma=False,
    )
```

```python
import functools

import jax
import jax.numpy as jnp
from jax import lax
from jax.experimental import pallas as pl
from jax.experimental.pallas import tpu as pltpu
from jax.sharding import PartitionSpec as P

HEAD_SIZE = 128
BLK = 128
LOC = 3
REM = 7
FEAT = 4096
LOW = -1e30

epsilon = 1e-06
softmax_scale = 1.0 / HEAD_SIZE**0.5

NT = (((1,), (1,)), ((), ()))
NN = (((1,), (0,)), ((), ()))
TN = (((0,), (0,)), ((), ()))


def dot(a, b, dims):
    return lax.dot_general(a, b, dims, preferred_element_type=jnp.float32)


def head_columns(h):
    return pl.ds(pl.multiple_of(h * HEAD_SIZE, HEAD_SIZE), HEAD_SIZE)


def blocks(first, count=1):
    return slice(first * BLK, (first + count) * BLK)


def pick_kernel(
    nblocks, me_ref, pattern_hbm, key_hbm, value_hbm, own_ref, start_ref, pattern_ref, key_ref, value_ref, sems
):
    copies = [
        pltpu.make_async_copy(source, target, sems.at[i])
        for i, (source, target) in enumerate(
            [(pattern_hbm, pattern_ref), (key_hbm, key_ref), (value_hbm, value_ref)]
        )
    ]
    for copy in copies:
        copy.start()
    copies[0].wait()
    pattern = pattern_ref[...]
    low = me_ref[0] * nblocks
    row = lax.broadcasted_iota(jnp.int32, pattern.shape, 1)
    inside = (pattern >= low) & (pattern < low + nblocks)
    others = (row < low) | (row >= low + nblocks)
    offset = jnp.where(inside & others, pattern - low, 0).astype(jnp.float32)
    start = pl.multiple_of(jnp.max(offset).astype(jnp.int32) * BLK, BLK)
    start_ref[0] = start
    copies[1].wait()
    copies[2].wait()
    own_ref[:BLK] = key_ref[pl.ds(start, BLK)]
    own_ref[BLK:] = value_ref[pl.ds(start, BLK)]


def gather_rows(cat_ref, pieces, cols):
    at = 0
    for piece, rows in pieces:
        size = rows.stop - rows.start
        cat_ref[at : at + size] = piece[rows, cols]
        at += size


def keys_of(slots):
    return [(slot, blocks(0)) for slot in slots]


def values_of(slots):
    return [(slot, blocks(1)) for slot in slots]


def is_listed(nblocks, ranges_ref, pattern_ref, g, local=None, place=None):
    low = ranges_ref[0] * nblocks
    listed = None
    for i in range(LOC) if place is None else range(LOC, LOC + REM):
        entry = pattern_ref[i, low + g]
        same = entry == low + local if place is None else entry // nblocks == ranges_ref[place]
        listed = same if listed is None else listed | same
    return jnp.where(listed, 0.0, LOW)


def biased(scores, biases):
    parts = [scores[:, blocks(j)] for j in range(len(biases))]
    parts = [p if bias is None else p + bias for p, bias in zip(parts, biases)]
    return jnp.concatenate(parts, axis=1)


def first_scores_kernel(nblocks, far_bias, ranges_ref, pattern_ref, q_ref, k_ref, *refs):
    slots = refs[:-4]
    p_ref, peak_ref, total_ref, cat_ref = refs[-4:]
    listed = functools.partial(is_listed, nblocks, ranges_ref, pattern_ref)
    biases = [
        [listed(g, local=j) for j in range(nblocks)]
        + [listed(g, place=1 + j) if far_bias else None for j in range(len(slots))]
        for g in range(nblocks)
    ]

    @pl.loop(0, p_ref.shape[0], unroll=4)
    def _(h):
        cols = head_columns(h)
        gather_rows(cat_ref, [(k_ref, blocks(0, nblocks))] + keys_of(slots), cols)
        for g in range(nblocks):
            rows = blocks(g)
            scores = dot(q_ref[rows, cols], cat_ref[...], NT) * softmax_scale
            scores = biased(scores, biases[g])
            peak = jnp.max(scores, axis=1, keepdims=True)
            expo = jnp.exp(scores - peak)
            total = jnp.sum(expo, axis=1, keepdims=True)
            p_ref[h, rows] = expo.astype(p_ref.dtype)
            peak_ref[h, rows] = jnp.broadcast_to(peak, (BLK, HEAD_SIZE))
            total_ref[h, rows] = jnp.broadcast_to(total, (BLK, HEAD_SIZE))


def first_attend_kernel(nblocks, p_ref, v_ref, *refs):
    slots = refs[:-2]
    o_ref, cat_ref = refs[-2:]

    @pl.loop(0, p_ref.shape[0], unroll=4)
    def _(h):
        cols = head_columns(h)
        gather_rows(cat_ref, [(v_ref, blocks(0, nblocks))] + values_of(slots), cols)
        o_ref[:, cols] = dot(p_ref[h], cat_ref[...], NN)


def later_biases(nblocks, far_bias, at, count, ranges_ref, pattern_ref):
    if not far_bias:
        return None
    listed = functools.partial(is_listed, nblocks, ranges_ref, pattern_ref)
    return [[listed(g, place=at + j) for j in range(count)] for g in range(nblocks)]


def later_scores(q, keys, biases):
    scores = dot(q, keys, NT) * softmax_scale
    if biases is None:
        return scores
    parts = [biased(scores[blocks(g)], biases[g]) for g in range(len(biases))]
    return jnp.concatenate(parts, axis=0)


def wide(x, like):
    return x if like.shape == x.shape else jnp.concatenate([x] * (like.shape[1] // BLK), axis=1)


def second_kernel(nblocks, far_bias, at, ranges_ref, pattern_ref, q_ref, peak_in, total_in, o_in, *refs):
    slots = refs[:-7]
    p_ref, shrink_ref, peak_ref, total_ref, o_ref, key_cat, value_cat = refs[-7:]
    biases = later_biases(nblocks, far_bias, at, len(slots), ranges_ref, pattern_ref)

    @pl.loop(0, p_ref.shape[0], unroll=True)
    def _(h):
        cols = head_columns(h)
        gather_rows(key_cat, keys_of(slots), cols)
        gather_rows(value_cat, values_of(slots), cols)
        scores = later_scores(q_ref[:, cols], key_cat[...], biases)
        old = peak_in[h]
        peak = jnp.maximum(old, jnp.max(scores, axis=1, keepdims=True))
        shrink = jnp.exp(old - peak)
        expo = jnp.exp(scores - wide(peak, scores))
        expo16 = expo.astype(p_ref.dtype)
        p_ref[h] = expo16
        shrink_ref[h] = shrink
        peak_ref[h] = peak
        total_ref[h] = total_in[h] * shrink + jnp.sum(expo, axis=1, keepdims=True)
        o_ref[:, cols] = o_in[:, cols] * shrink + dot(expo16, value_cat[...], NN)


def third_kernel(
    nblocks,
    far_bias,
    at,
    ranges_ref,
    pattern_ref,
    q_ref,
    peak_ref,
    total_ref,
    shrink_ref,
    o_in,
    grad_ref,
    gain_ref,
    slot_ref,
    p_ref,
    scale_a_ref,
    scale_b_ref,
    o_ref,
    stat_ref,
    square_ref,
    cross_ref,
):
    biases = later_biases(nblocks, far_bias, at, 1, ranges_ref, pattern_ref)
    square_ref[...] = jnp.zeros_like(square_ref)
    cross_ref[...] = jnp.zeros_like(cross_ref)

    @pl.loop(0, p_ref.shape[0], unroll=True)
    def _(h):
        cols = head_columns(h)
        scores = later_scores(q_ref[:, cols], slot_ref[blocks(0), cols], biases)
        old = peak_ref[h]
        peak = jnp.maximum(old, jnp.max(scores, axis=1, keepdims=True))
        shrink = jnp.exp(old - peak)
        expo = jnp.exp(scores - peak)
        total = total_ref[h] * shrink + jnp.sum(expo, axis=1, keepdims=True)
        inverse = 1.0 / total
        prob = (expo * inverse).astype(p_ref.dtype)
        p_ref[h] = prob
        scale = shrink * inverse
        scale_b_ref[h] = scale
        scale_a_ref[h] = scale * shrink_ref[h]
        out = o_in[:, cols] * scale + dot(prob, slot_ref[blocks(1), cols], NN)
        o_ref[:, cols] = out
        scaled = grad_ref[:, cols].astype(jnp.float32) * gain_ref[:, cols]
        square_ref[...] += out * out
        cross_ref[...] += scaled * out

    squares = jnp.sum(square_ref[...].T, axis=0, keepdims=True)
    cross = jnp.sum(cross_ref[...].T, axis=0, keepdims=True)
    for g in range(nblocks):
        stat_ref[g : g + 1] = squares[:, blocks(g)]
        stat_ref[nblocks + g : nblocks + g + 1] = cross[:, blocks(g)]


def score_grad(d, delta, scales, value_cat, parts):
    dprob = dot(d, value_cat, NT)
    result = []
    for j, (prob, part) in enumerate(parts):
        term = prob.astype(jnp.float32) * (dprob[:, blocks(j)] - delta)
        term = term if scales[part] is None else term * scales[part]
        result.append(term.astype(jnp.bfloat16))
    return jnp.concatenate(result, axis=1)


def put_slots(slots, prob_parts, d_parts, dscore, q, cols):
    for j, (slot, (prob, part)) in enumerate(zip(slots, prob_parts)):
        key_term = dot(dscore[:, blocks(j)], q, TN) * softmax_scale
        slot[:BLK, cols] = key_term.astype(slot.dtype)
        slot[BLK:, cols] = dot(prob, d_parts[part], TN).astype(slot.dtype)


def take(places, p_refs, h):
    return [(p_refs[part][h, :, blocks(j)], part) for part, j in places]


def grad_out_kernel(
    place,
    q_ref,
    stat_ref,
    o_ref,
    grad_ref,
    gain_ref,
    scale_a_ref,
    scale_b_ref,
    p_ref,
    slot_ref,
    normed_ref,
    d_ref,
    d_a_ref,
    d_b_ref,
    delta_ref,
    dq_ref,
    out_ref,
    inverse_ref,
    factor_ref,
):
    tokens = o_ref.shape[0]
    stats = jnp.sum(stat_ref[...], axis=0)
    rows = [jnp.broadcast_to(stats[g : g + 1], (HEAD_SIZE, BLK)).T for g in range(stats.shape[0])]
    squares = jnp.concatenate(rows[: tokens // BLK], axis=0)
    cross = jnp.concatenate(rows[tokens // BLK :], axis=0)
    inverse = lax.rsqrt(squares / FEAT + epsilon)
    inverse_ref[...] = inverse
    factor_ref[...] = inverse * inverse * inverse * cross / FEAT

    @pl.loop(0, p_ref.shape[0], unroll=True)
    def _(h):
        cols = head_columns(h)
        out = o_ref[:, cols]
        inverse = inverse_ref[...]
        gain = gain_ref[:, cols]
        scaled = grad_ref[:, cols].astype(jnp.float32) * gain
        normed_ref[:, cols] = (out * inverse * gain).astype(normed_ref.dtype)
        d_attended = inverse * scaled - out * factor_ref[...]
        d = d_attended.astype(d_ref.dtype)
        d_ref[:, cols] = d
        d_a_ref[:, cols] = (d_attended * scale_a_ref[h]).astype(d_ref.dtype)
        d_b_ref[:, cols] = (d_attended * scale_b_ref[h]).astype(d_ref.dtype)
        delta = jnp.sum(d.astype(jnp.float32) * out, axis=1, keepdims=True)
        delta = jnp.broadcast_to(delta, out.shape)
        delta_ref[h] = delta
        parts = take([place], (None, None, p_ref), h)
        dscore = score_grad(d, delta, (None, None, None), slot_ref[blocks(1), cols], parts)
        dq_ref[:, cols] = dot(dscore, slot_ref[blocks(0), cols], NN)
        put_slots([out_ref], parts, (None, None, d), dscore, q_ref[:, cols], cols)


def slots_kernel(
    places, q_ref, d_ref, d_a_ref, d_b_ref, delta_ref, scale_a_ref, scale_b_ref, pa_ref, pb_ref, dq_in, *refs
):
    n = len(places)
    dq_ref = refs[n]
    outs = refs[n + 1 : 2 * n + 1]
    key_cat, value_cat = refs[2 * n + 1 :]

    @pl.loop(0, pa_ref.shape[0], unroll=True)
    def _(h):
        cols = head_columns(h)
        gather_rows(key_cat, keys_of(refs[:n]), cols)
        gather_rows(value_cat, values_of(refs[:n]), cols)
        parts = take(places, (pa_ref, pb_ref), h)
        scales = (scale_a_ref[h], scale_b_ref[h])
        dscore = score_grad(d_ref[:, cols], delta_ref[h], scales, value_cat[...], parts)
        dq_ref[:, cols] = dq_in[:, cols] + dot(dscore, key_cat[...], NN)
        put_slots(outs, parts, (d_a_ref[:, cols], d_b_ref[:, cols]), dscore, q_ref[:, cols], cols)


def local_kernel(
    nblocks,
    start_ref,
    q_ref,
    k_ref,
    v_ref,
    d_ref,
    scaled_d_ref,
    delta_ref,
    scale_ref,
    pa_ref,
    dq_in,
    dq_ref,
    key_local_ref,
    value_local_ref,
    export_ref,
    key_term,
    value_term,
):
    start = pl.multiple_of(start_ref[0], BLK)
    tokens = q_ref.shape[0]

    @pl.loop(0, pa_ref.shape[0], unroll=True)
    def _(h):
        cols = head_columns(h)
        parts = [(pa_ref[h, :, blocks(j)], 0) for j in range(nblocks)]
        dscore = score_grad(d_ref[:, cols], delta_ref[h], (scale_ref[h],), v_ref[:, cols], parts)
        dq = dq_in[:, cols] + dot(dscore, k_ref[:, cols], NN)
        dq_ref[:, cols] = (dq * softmax_scale).astype(dq_ref.dtype)
        key_term[...] = dot(dscore, q_ref[:, cols], TN) * softmax_scale
        value_term[...] = dot(pa_ref[h, :, :tokens], scaled_d_ref[:, cols], TN)
        key_local_ref[:, cols] = key_term[...].astype(key_local_ref.dtype)
        value_local_ref[:, cols] = value_term[...].astype(value_local_ref.dtype)
        export_ref[:BLK, cols] = key_term[pl.ds(start, BLK)]
        export_ref[BLK:, cols] = value_term[pl.ds(start, BLK)]


def finish_kernel(start_ref, mine_ref, *refs):
    came = refs[:-4]
    key_out, value_out = refs[-2:]
    total = mine_ref[...]
    for term in came:
        total = total + term[...].astype(jnp.float32)
    key_out[...] = total[:BLK].astype(key_out.dtype)
    value_out[...] = total[BLK:].astype(value_out.dtype)


def after(x, *earlier):
    return lax.optimization_barrier((x, earlier))[0]


def shards(queries, keys, values, gain, grad_out, pattern):
    n_seq = lax.axis_size("seq")
    far = n_seq // 2
    myself = lax.axis_index("seq")
    tokens, width = queries.shape
    heads = width // HEAD_SIZE
    nblocks = tokens // BLK
    a, b = myself // 2, myself % 2
    bf16, f32 = jnp.bfloat16, jnp.float32
    pattern = pattern.T
    inner, outer = (1, 2), (0, 3)

    def move(x, to, among=None):
        among = range(far) if among is None else among
        return lax.ppermute(x, "seq", [(i * 2 + j, to(i) * 2 + j) for i in among for j in range(2)])

    def swap(x):
        return lax.ppermute(x, "seq", [(i, i ^ 1) for i in range(n_seq)])

    half = far // 2
    is_inner = (a == 1) | (a == 2)
    sources = [a ^ k for k in range(1, far)]
    if far == 4:
        sources[1:] = [jnp.where(is_inner, a ^ 3, a ^ 2), jnp.where(is_inner, a ^ 2, a ^ 3)]
    near_ranges = [s * 2 + b for s in sources]
    mate_ranges = [s * 2 + 1 - b for s in [a] + sources]
    ranges = jnp.stack(
        [myself] + near_ranges[:-1] + mate_ranges[:half] + near_ranges[-1:] + mate_ranges[half:]
    )
    far_bias = n_seq - 1 != REM

    smem = pl.BlockSpec(memory_space=pltpu.SMEM)
    vmem = pl.BlockSpec(memory_space=pltpu.VMEM)
    shape = jax.ShapeDtypeStruct

    def call(name, kernel, inputs, out_shape, scratch=(), in_smem=(), out_smem=(), cost=10**8):
        single = not isinstance(out_shape, list)
        n_out = 1 if single else len(out_shape)
        out_specs = [smem if i in out_smem else vmem for i in range(n_out)]
        return pl.pallas_call(
            kernel,
            in_specs=[smem if i in in_smem else vmem for i in range(len(inputs))],
            out_specs=out_specs[0] if single else out_specs,
            out_shape=out_shape,
            scratch_shapes=[pltpu.VMEM(*s) for s in scratch],
            compiler_params=pltpu.CompilerParams(vmem_limit_bytes=12 * 1024 * 1024),
            cost_estimate=pl.CostEstimate(flops=cost * 1000, bytes_accessed=cost, transcendentals=0),
            name=name,
        )(*inputs)

    hbm = pl.BlockSpec(memory_space=pltpu.MemorySpace.HBM)
    own, start_vec = pl.pallas_call(
        functools.partial(pick_kernel, nblocks),
        in_specs=[smem, hbm, hbm, hbm],
        out_specs=[vmem, smem],
        out_shape=[shape((2 * BLK, width), bf16), shape((1,), jnp.int32)],
        scratch_shapes=[
            pltpu.VMEM(pattern.shape, jnp.int32),
            pltpu.VMEM((tokens, width), bf16),
            pltpu.VMEM((tokens, width), bf16),
            pltpu.SemaphoreType.DMA((3,)),
        ],
        name="pick",
    )(myself.reshape(1), pattern, keys, values)

    if far == 4:
        m0 = swap(own)
        s1 = move(own, lambda i: i ^ 1)
        mid1 = move(own, lambda i: i ^ 3, inner)
        m1 = swap(after(s1, m0))
        mid2 = move(s1, lambda i: i ^ 3, inner)
        end2 = move(mid1, lambda i: i ^ 1, inner)
        s2 = jnp.where(is_inner, mid1, end2)
        m2 = swap(after(s2, m1))
        end3 = move(mid2, lambda i: i ^ 1, inner)
        s3 = jnp.where(is_inner, mid2, end3)
        m3 = swap(after(s3, m2))
        near, mates = [s1, s2, s3], [m0, m1, m2, m3]
    else:
        near = [move(own, lambda i, k=k: i ^ k) for k in range(1, far)]
        mates = [swap(x) for x in [own] + near]
    slots_a = near[:-1] + mates[:half]
    slots_b = near[-1:] + mates[half:-1]
    cols_a = tokens + len(slots_a) * BLK
    cols_b = len(slots_b) * BLK
    gain_row = gain.reshape(1, width)
    rows_shape = shape((heads, tokens, HEAD_SIZE), f32)
    wide16, wide32 = shape((tokens, width), bf16), shape((tokens, width), f32)

    prob_a, peak_a, total_a = call(
        "first_scores",
        functools.partial(first_scores_kernel, nblocks, far_bias),
        [ranges, pattern, queries, keys, *slots_a],
        [shape((heads, tokens, cols_a), bf16), rows_shape, rows_shape],
        [((cols_a, HEAD_SIZE), bf16)],
        in_smem=(0, 1),
    )
    attended = call(
        "first_attend",
        functools.partial(first_attend_kernel, nblocks),
        [prob_a, values, *slots_a],
        wide32,
        [((cols_a, HEAD_SIZE), bf16)],
    )
    prob_b, shrink, peak_b, total_b, attended = call(
        "second",
        functools.partial(second_kernel, nblocks, far_bias, 1 + len(slots_a)),
        [ranges, pattern, queries, peak_a, total_a, attended, *slots_b],
        [shape((heads, tokens, cols_b), bf16), rows_shape, rows_shape, rows_shape, wide32],
        [((cols_b, HEAD_SIZE), bf16)] * 2,
        in_smem=(0, 1),
        cost=1000,
    )
    prob_c, scale_a, scale_b, attended, stats = call(
        "third",
        functools.partial(third_kernel, nblocks, far_bias, 1 + len(slots_a) + len(slots_b)),
        [ranges, pattern, queries, peak_b, total_b, shrink, attended, grad_out, gain_row, mates[-1]],
        [shape((heads, tokens, BLK), bf16), rows_shape, rows_shape, wide32, shape((2 * nblocks, BLK), f32)],
        [((tokens, HEAD_SIZE), f32)] * 2,
        in_smem=(0, 1),
    )

    stats = lax.all_gather(stats, "head")

    near_places = [(0, nblocks + k) for k in range(far - 2)] + [(1, 0)]
    mate_places = [(0, nblocks + far - 2 + k) for k in range(half)]
    mate_places += [(1, 1 + k) for k in range(far - half - 1)] + [(2, 0)]
    pair = shape((2 * BLK, width), bf16)

    def cats(n):
        return [((n * BLK, HEAD_SIZE), bf16)] * 2

    normed, d_attended, d_a, d_b, delta, dq, mate_last = call(
        "grad_out",
        functools.partial(grad_out_kernel, mate_places[-1]),
        [queries, stats, attended, grad_out, gain_row, scale_a, scale_b, prob_c, mates[-1]],
        [wide16, wide16, wide16, wide16, rows_shape, wide32, pair],
        [((tokens, HEAD_SIZE), f32)] * 2,
    )

    def slot_terms(name, places, slots, dq):
        n = len(slots)
        return call(
            name,
            functools.partial(slots_kernel, places),
            [queries, d_attended, d_a, d_b, delta, scale_a, scale_b, prob_a, prob_b, dq, *slots],
            [wide32] + [pair] * n,
            cats(n),
        )

    def add(*terms):
        return sum(t.astype(f32) for t in terms).astype(bf16)

    y_last = swap(mate_last)
    if far == 4:
        dq, mate2, mate1, near3, near2 = slot_terms(
            "terms_far",
            [mate_places[2], mate_places[1], near_places[2], near_places[1]],
            [mates[2], mates[1], near[2], near[1]],
            dq,
        )
        y2 = swap(mate2)
        y1 = swap(mate1)
        dq, near1, mate0 = slot_terms(
            "terms_near", [near_places[0], mate_places[0]], [near[0], mates[0]], dq
        )
        c3 = add(after(near3, near1), y_last)
        end3 = move(c3, lambda i: i ^ 1, outer)
        far3 = move(add(c3, end3), lambda i: i ^ 2, inner)
        dq = after(dq, c3)
    else:
        dq, mate0, near_last = slot_terms(
            "terms_ends",
            [mate_places[0], near_places[-1]],
            [mates[0], near[-1]],
            dq,
        )
        came = [swap(mate0), move(add(near_last, y_last), lambda i: i ^ (far - 1))]
        for k in range(1, far - 1):
            dq, mate_k, near_k = slot_terms(
                "terms",
                [mate_places[k], near_places[k - 1]],
                [mates[k], near[k - 1]],
                dq,
            )
            came.append(move(add(near_k, swap(mate_k)), lambda i, k=k: i ^ k))

    grad_queries, key_local, value_local, mine = call(
        "terms_local",
        functools.partial(local_kernel, nblocks),
        [start_vec, queries, keys, values, d_attended, d_a, delta, scale_a, prob_a, dq],
        [wide16, wide16, wide16, shape((2 * BLK, width), f32)],
        [((tokens, HEAD_SIZE), f32)] * 2,
        in_smem=(0,),
        cost=1000,
    )
    if far == 4:
        c2 = add(after(near2, mine), y2)
        end2 = move(c2, lambda i: i ^ 1, outer)
        c1 = add(near1, y1)
        near_came = move(c1, lambda i: i ^ 1)
        mid2 = move(add(c2, after(end2, far3)), lambda i: i ^ 3, inner)
        y0 = swap(after(mate0, y1))
        came = [far3, mid2, y0, near_came]
    at = 2 + len(came)
    block = pl.BlockSpec((BLK, width), lambda i, place: (place[0], 0))
    grad_keys, grad_values = pl.pallas_call(
        finish_kernel,
        grid_spec=pltpu.PrefetchScalarGridSpec(
            num_scalar_prefetch=1,
            grid=(1,),
            in_specs=[vmem] * (1 + len(came)) + [hbm, hbm],
            out_specs=[block, block],
        ),
        out_shape=[wide16, wide16],
        input_output_aliases={at: 0, at + 1: 1},
        name="finish",
    )(start_vec // BLK, mine, *came, key_local, value_local)
    return normed, grad_queries, grad_keys, grad_values


def solution(mesh):
    split = P("seq", "head")
    return jax.shard_map(
        shards,
        mesh=mesh,
        in_specs=(split, split, split, P("head"), split, P()),
        out_specs=(split, split, split, split),
        check_vma=False,
    )
```
